512 devices in a mesh: sec: 16 (over z), tile: 32 (over y, x, core).
Axes of the slice: x: 4, y: 4, z: 16, core: 2. Of those that a mesh axis runs over, the one named last changes fastest.
Arguments:
- object_slab: float32 [32, 2, 8192, 256], P('sec', None, 'tile')
- probe: float32 [2, 2, 128, 128], replicated, may hold values from -4 to 4
- amplitudes: bfloat16 [256, 128, 128], P('tile'), may hold values from 0.19921875 to 2
- offsets: int32 [256, 2], P('tile'), may hold values from 0 to 128
- counts: int32 [32], P('tile'), may hold values from 1 to 8, as said below
Outputs:
- object_grad: float32 [32, 2, 8192, 256], P('sec', None, 'tile')
- probe_grad: float32 [65536], P(('sec', 'tile'))
The draws below stay inside these ranges and needn't reach their ends.
Inputs may be any that keep to these rules, and one draw needn't show every extreme that they name: The first counts[q] slots of tile q are live; some tile has all 8 slots live.
All inputs are finite; a program needn't handle non-finite values.
Results may differ from the reference program's by a relative error of at most 0.04.
Values may be sent and summed in bfloat16 or wider, within the bound.
A program may use at most 64 MiB of HBM per device.

```python
import jax
import jax.numpy as jnp
from jax import lax

PR = 128
MODES = 2
SL_DEV = 2
CAP = 8
TILE = 256
SLICES = 32
POSITIONS = 256
N_SEC = 16
N_TILE = 32


def draw_object_slab(key, part):
    key = jax.random.fold_in(key, 11)
    key_real, key_imag = jax.random.split(key)
    shape = (SLICES, N_TILE * TILE, TILE)
    real_part = 1.0 + 0.05 * jax.random.normal(key_real, shape, jnp.float32)
    imag_part = 0.2 * jax.random.normal(key_imag, shape, jnp.float32)
    return jnp.stack([real_part, imag_part], axis=1)


def draw_counts(key, part):
    key = jax.random.fold_in(key, 12)
    key_base, key_full = jax.random.split(key)
    drawn = jax.random.randint(key_base, (N_TILE,), 1, CAP + 1)
    full_tile = jax.random.randint(key_full, (), 0, N_TILE)
    return jnp.where(jnp.arange(N_TILE) == full_tile, CAP, drawn).astype(jnp.int32)


def with_ends(values, own_key, low, largest):
    longest = values.shape.index(max(values.shape))
    spots = []
    for shift in (0, 1):
        where = [jax.random.randint(jax.random.fold_in(own_key, axis), (), 0, length) for axis, length in enumerate(values.shape)]
        where[longest] = (where[longest] + shift) % values.shape[longest]
        spots.append(tuple(where))
    return values.at[spots[0]].set(low).at[spots[1]].set(largest)


def levels(stream_key, extent, cuts, least, largest):
    loudness = 1.0
    for dim, shards_of in cuts:
        heights = jax.random.uniform(jax.random.fold_in(jax.random.fold_in(stream_key, 6), dim), (shards_of,), jnp.float32, least / len(cuts), largest / len(cuts))
        loudness = loudness * jnp.repeat(jnp.exp(heights), extent[dim] // shards_of).reshape((-1,) + (1,) * (len(extent) - 1 - dim))
    return loudness


def scatter_about(key, extent, scale, limit, kind=jnp.bfloat16):
    return jnp.clip(scale * jax.random.normal(key, extent, jnp.float32), -limit, limit).astype(kind)


def setup_inputs(seed: int = 0) -> dict:
    splits = jax.random.split(jax.random.key(seed), 6)
    object_slab = draw_object_slab(jax.random.fold_in(splits[5], 71), 0)
    probe = scatter_about(splits[1], (MODES, 2, PR, PR), 0.5, 4.0, jnp.float32)
    amplitudes = jnp.clip(0.19921875 + 1.8007812 * jax.random.uniform(splits[2], (POSITIONS, PR, PR), jnp.float32) ** levels(splits[2], (POSITIONS, PR, PR), ((0, 32),), -0.2, 0.2), 0.19921875, 2.0).astype(jnp.bfloat16)
    offsets = with_ends(jax.random.randint(splits[3], (POSITIONS, 2), 0, TILE - PR + 1), jax.random.fold_in(splits[3], 1), 0, TILE - PR).astype(jnp.int32)
    counts = draw_counts(jax.random.fold_in(splits[5], 71), 0)
    return dict(object_slab=object_slab, probe=probe, amplitudes=amplitudes, offsets=offsets, counts=counts)


PHASE_SCALE = 20.0

def propagator(length):
    frequency = jnp.fft.fftfreq(length)
    factors = jnp.exp(-1j * PHASE_SCALE * frequency * frequency)
    return factors[:, None] * factors[None, :]

def propagate(field_in, kernel):
    return jnp.fft.ifft2(jnp.fft.fft2(field_in) * kernel)

def rounded(field_in):
    real_part = jnp.real(field_in).astype(jnp.bfloat16)
    imag_part = jnp.imag(field_in).astype(jnp.bfloat16)
    real_part, imag_part = lax.optimization_barrier((real_part, imag_part))
    return real_part.astype(jnp.float32) + 1j * imag_part.astype(jnp.float32)

def reference(object_slab, probe, amplitudes, offsets, counts):
    kernel = propagator(PR)
    tiles_object = jnp.moveaxis(object_slab.reshape(SLICES, 2, N_TILE, TILE, TILE), 2, 0)
    tiles_amps = amplitudes.reshape(N_TILE, CAP, PR, PR)
    tiles_corners = offsets.reshape(N_TILE, CAP, 2)
    incident = probe[:, 0] + 1j * probe[:, 1]
    anchor = jnp.zeros((), jnp.int32)

    def one_tile(operands):
        tile_slab, tile_amps, corners, live_count = operands

        def cut_window(corner_pair):
            return lax.dynamic_slice(tile_slab, (anchor, anchor, corner_pair[0], corner_pair[1]), (SLICES, 2, PR, PR))
        patches = jax.vmap(cut_window)(corners)
        transmission = patches[:, :, 0] + 1j * patches[:, :, 1]
        wave_field = jnp.broadcast_to(incident[None], (CAP, MODES, PR, PR))
        entering = []
        for section in range(N_SEC):
            for stratum in range(SL_DEV):
                layer_index = section * SL_DEV + stratum
                entering.append(wave_field)
                wave_field = propagate(transmission[:, layer_index][:, None] * wave_field, kernel)
            if section < N_SEC - 1:
                wave_field = rounded(wave_field)
        far_field = jnp.fft.fft2(wave_field, norm='ortho')
        intensity = lax.optimization_barrier(jnp.sum(jnp.real(far_field) ** 2 + jnp.imag(far_field) ** 2, axis=1))
        modelled = jnp.sqrt(intensity + 0.25)
        live_mask = (jnp.arange(CAP, dtype=jnp.int32) < live_count).astype(jnp.float32)
        factor = 2.0 * (1.0 - tile_amps.astype(jnp.float32) / modelled) * live_mask[:, None, None]
        gradient = jnp.fft.ifft2(factor[:, None] * far_field, norm='ortho')
        pieces = [None] * SLICES
        for section in reversed(range(N_SEC)):
            for stratum in reversed(range(SL_DEV)):
                layer_index = section * SL_DEV + stratum
                middle = propagate(gradient, jnp.conj(kernel))
                pieces[layer_index] = lax.optimization_barrier(jnp.sum(jnp.conj(entering[layer_index]) * middle, axis=1))
                gradient = jnp.conj(transmission[:, layer_index])[:, None] * middle
            if section > 0:
                gradient = rounded(gradient)
        stacked = jnp.stack(pieces, axis=1)
        patch_grads = jnp.stack([jnp.real(stacked), jnp.imag(stacked)], axis=2)

        def accumulate(position, total):
            corner = (anchor, anchor, corners[position, 0], corners[position, 1])
            current = lax.dynamic_slice(total, corner, (SLICES, 2, PR, PR))
            return lax.dynamic_update_slice(total, current + patch_grads[position], corner)
        slab_grad = lax.fori_loop(0, CAP, accumulate, jnp.zeros((SLICES, 2, TILE, TILE), jnp.float32))
        probe_part = lax.optimization_barrier(jnp.sum(gradient, axis=0))
        return (slab_grad, jnp.stack([jnp.real(probe_part), jnp.imag(probe_part)], axis=1))
    slab_grads, probe_parts = lax.map(one_tile, (tiles_object, tiles_amps, tiles_corners, counts))
    object_grad = jnp.moveaxis(slab_grads, 0, 2).reshape(SLICES, 2, N_TILE * TILE, TILE)
    probe_grad = lax.optimization_barrier(jnp.sum(probe_parts, axis=0)).reshape(-1)
    return (object_grad, probe_grad)
```

```python
import functools

import jax
import jax.numpy as jnp
import ml_dtypes
import numpy as np
from jax import lax
from jax.experimental import pallas as pl
from jax.experimental.pallas import tpu as pltpu
from jax.sharding import PartitionSpec as P

PHASE_SCALE = 20.0
F32 = jnp.float32
BF16 = jnp.bfloat16
MESH = pl.DeviceIdType.MESH


def real_forms(matrix):
    re, im = matrix.real, matrix.imag
    left = np.block([[re, -im], [im, re]])
    right = np.block([[re, im], [-im, re]])
    pieces = []
    for table in (right, left):
        table = table.astype(np.float32)
        high = table.astype(ml_dtypes.bfloat16)
        low = (table - high.astype(np.float32)).astype(ml_dtypes.bfloat16)
        pieces += [high, low]
    return pieces


def tables(length):
    index = np.arange(length)
    dft = np.exp(-2j * np.pi * (np.outer(index, index) % length) / length)
    frequency = np.where(index < (length + 1) // 2, index, index - length) / length
    phases = np.exp(-1j * PHASE_SCALE * frequency * frequency)
    propagator = (dft.conj() @ (phases[:, None] * dft)) / length
    return np.stack(real_forms(propagator) + real_forms(dft / np.sqrt(length)))


def split(value):
    high = value.astype(BF16)
    return high, (value - high.astype(F32)).astype(BF16)


def dot(a, b):
    return jnp.dot(a, b, preferred_element_type=F32)


def two_sided(tab_ref, right, left, re, im):
    n = re.shape[0]
    high, low = split(jnp.concatenate([re, im], axis=1))
    right_high = tab_ref[right]
    half = dot(high, right_high) + dot(low, right_high) + dot(high, tab_ref[right + 1])
    high, low = split(jnp.concatenate([half[:, :n], half[:, n:]], axis=0))
    both = dot(tab_ref[left], jnp.concatenate([high, low], axis=1))
    out = both[:, :n] + both[:, n:] + dot(tab_ref[left + 1], high)
    return out[:n], out[n:]


def one_hot(rows, columns, row_shift, column_shift):
    down = lax.broadcasted_iota(jnp.int32, (rows, columns), 0) + row_shift
    across = lax.broadcasted_iota(jnp.int32, (rows, columns), 1) + column_shift
    return jnp.where(down == across, 1.0, 0.0).astype(BF16)


def kernel(
    sections, tiles,
    slab_ref, probe_ref, amps_ref, offsets_ref, counts_ref, tab_ref,
    grad_ref, probe_out_ref,
    slab_parts, win, entering, mid, exits, seeds, patch, probe_acc,
    send_f, recv_f, send_b, recv_b, pieces, sums,
    sem_sf, sem_rf, sem_sb, sem_rb, sem_ps, sem_pr, sem_zs, sem_zr,
):
    n = probe_ref.shape[-1]
    tile_side = slab_ref.shape[-1]
    layers = slab_ref.shape[0]
    waves = send_f.shape[0]
    positions = waves // 2
    s = lax.axis_index("sec")
    t = lax.axis_index("tile")
    first, last = s == 0, s == sections - 1
    planes = [(l, c) for l in range(layers) for c in range(2)]

    barrier = pltpu.get_barrier_semaphore()

    def greet(sec, tile):
        pl.semaphore_signal(barrier, inc=1, device_id=(sec, tile), device_id_type=MESH)

    @pl.when(first)
    def _():
        greet(1, t)
        for other in range(tiles):
            @pl.when(other != t)
            def _():
                greet(0, other)

    @pl.when(s > 0)
    def _():
        greet(s - 1, t)

        @pl.when(s > 1)
        def _():
            greet(0, t)

        @pl.when(s < sections - 1)
        def _():
            greet(s + 1, t)

    for at, (l, c) in enumerate(planes):
        high, low = split(slab_ref[l, c])
        slab_parts[:, at * tile_side:(at + 1) * tile_side] = high
        shift = (at + len(planes)) * tile_side
        slab_parts[:, shift:shift + tile_side] = low
    grad_ref[...] = jnp.zeros_like(grad_ref)
    patch[...] = jnp.zeros_like(patch)
    probe_acc[...] = jnp.zeros_like(probe_acc)

    def cut(p):
        rows = one_hot(n, tile_side, offsets_ref[p, 0], 0)
        columns = one_hot(tile_side, n, 0, offsets_ref[p, 1])
        for at, (l, c) in enumerate(planes):
            value = None
            for part in (at, at + len(planes)):
                strip = dot(rows, slab_parts[:, part * tile_side:(part + 1) * tile_side]).astype(BF16)
                term = dot(strip, columns)
                value = term if value is None else value + term
            win[p, l, c] = value

    def place(p):
        rows = one_hot(tile_side, n, 0, offsets_ref[p, 0])
        columns = one_hot(n, tile_side, offsets_ref[p, 1], 0)
        for l, c in planes:
            high, low = split(patch[l, c])
            wide = jnp.concatenate([dot(high, columns).astype(BF16), dot(low, columns).astype(BF16)], axis=1)
            both = dot(rows, wide)
            grad_ref[l, c] += both[:, :tile_side] + both[:, tile_side:]
        patch[...] = jnp.zeros_like(patch)

    def copy_f(k):
        return pltpu.make_async_remote_copy(
            src_ref=send_f.at[k], dst_ref=recv_f.at[k], send_sem=sem_sf.at[k], recv_sem=sem_rf.at[k],
            device_id=(s + 1, t), device_id_type=MESH)

    def copy_b(k):
        return pltpu.make_async_remote_copy(
            src_ref=send_b.at[k], dst_ref=recv_b.at[k], send_sem=sem_sb.at[k], recv_sem=sem_rb.at[k],
            device_id=(s - 1, t), device_id_type=MESH)

    cut(0)

    @pl.when(first)
    def _():
        pl.semaphore_wait(barrier, sections - 1 + tiles - 1)

    @pl.when((s > 0) & (s < sections - 1))
    def _():
        pl.semaphore_wait(barrier, 2)

    @pl.when(last)
    def _():
        pl.semaphore_wait(barrier, 1)

    def forward(k):
        p, m = k // 2, k % 2

        @pl.when(first)
        def _():
            entering[...] = probe_ref[m]

        @pl.when(s > 0)
        def _():
            copy_f(k).wait_recv()
            entering[...] = recv_f[k].astype(F32)

        re, im = entering[0], entering[1]
        for l in range(layers):
            if l > 0:
                mid[k, 0] = re
                mid[k, 1] = im
            tr, ti = win[p, l, 0], win[p, l, 1]
            re, im = two_sided(tab_ref, 0, 2, tr * re - ti * im, tr * im + ti * re)
        send_f[k, 0] = re.astype(BF16)
        send_f[k, 1] = im.astype(BF16)

        @pl.when(s < sections - 1)
        def _():
            copy_f(k).start()

        exits[m, 0] = re
        exits[m, 1] = im

    def far(p):
        spectrum = [two_sided(tab_ref, 4, 6, exits[m, 0], exits[m, 1]) for m in range(2)]
        intensity = sum(re * re + im * im for re, im in spectrum)
        modelled = jnp.sqrt(intensity + 0.25)
        live = jnp.where(p < counts_ref[0], 2.0, 0.0)
        factor = live * (1.0 - amps_ref[p].astype(F32) / modelled)
        for m, (re, im) in enumerate(spectrum):
            seeds[m, 0], seeds[m, 1] = two_sided(tab_ref, 6, 4, factor * re, factor * im)

    def backward(k):
        p, m = k // 2, k % 2

        @pl.when(last)
        def _():
            entering[...] = seeds[m]

        @pl.when(s < sections - 1)
        def _():
            copy_b(k).wait_recv()
            entering[...] = recv_b[k].astype(F32)

        re, im = entering[0], entering[1]

        @pl.when(first)
        def _():
            entering[...] = probe_ref[m]

        @pl.when(s > 0)
        def _():
            entering[...] = recv_f[k].astype(F32)

        for l in reversed(range(layers)):
            re, im = two_sided(tab_ref, 2, 0, re, im)
            xr, xi = (entering[0], entering[1]) if l == 0 else (mid[k, 0], mid[k, 1])
            patch[l, 0] += xr * re + xi * im
            patch[l, 1] += xr * im - xi * re
            tr, ti = win[p, l, 0], win[p, l, 1]
            re, im = tr * re + ti * im, tr * im - ti * re
        send_b[k, 0] = re.astype(BF16)
        send_b[k, 1] = im.astype(BF16)

        @pl.when(s > 0)
        def _():
            copy_b(k).start()

        @pl.when(first)
        def _():
            groups = sections // 4
            for c, part in enumerate((re, im)):
                where = pl.ds((2 * m + c) * groups, groups)
                probe_acc[where] += part.reshape((groups,) + probe_acc.shape[1:])

        @pl.when(m == 1)
        def _():
            place(p)

    lag = jnp.minimum(waves, 2 + 5 * (sections - 1 - s))

    def turn(k, carry):
        @pl.when((k >= lag) & (k < lag + waves))
        def _():
            backward(k - lag)

        @pl.when(k < waves)
        def _():
            forward(k)

            @pl.when(last & (k % 2 == 1))
            def _():
                far(k // 2)

            @pl.when((k % 2 == 0) & (k < waves - 2))
            def _():
                cut(k // 2 + 1)

        return carry

    lax.fori_loop(0, 2 * waves, turn, 0)

    share = probe_acc.shape[1] // tiles

    def of_tile(other):
        return probe_acc.at[:, other] if share == 1 else probe_acc.at[:, pl.ds(other * share, share)]

    def copy_p(other):
        return pltpu.make_async_remote_copy(
            src_ref=of_tile(other), dst_ref=pieces.at[t], send_sem=sem_ps.at[other], recv_sem=sem_pr.at[t],
            device_id=(0, other), device_id_type=MESH)

    def arrival_p(other):
        return pltpu.make_async_remote_copy(
            src_ref=of_tile(0), dst_ref=pieces.at[other], send_sem=sem_ps.at[other], recv_sem=sem_pr.at[other],
            device_id=(0, other), device_id_type=MESH)

    def copy_z(sec):
        return pltpu.make_async_remote_copy(
            src_ref=sums.at[sec], dst_ref=sums.at[0], send_sem=sem_zs.at[sec], recv_sem=sem_zr,
            device_id=(sec, t), device_id_type=MESH)

    @pl.when(first)
    def _():
        for other in range(tiles):
            @pl.when(other != t)
            def _():
                copy_p(other).start()

            @pl.when(other == t)
            def _():
                pieces[other] = of_tile(other)[...]
        for other in range(tiles):
            @pl.when(other != t)
            def _():
                arrival_p(other).wait_recv()
        total = pieces[0]
        for other in range(1, tiles):
            total = total + pieces[other]
        for sec in range(sections):
            sums[sec] = jnp.broadcast_to(total[sec], sums.shape[1:])
        for sec in range(1, sections):
            copy_z(sec).start()
        for other in range(tiles):
            @pl.when(other != t)
            def _():
                copy_p(other).wait_send()
        for sec in range(1, sections):
            copy_z(sec).wait_send()

    @pl.when(s > 0)
    def _():
        copy_z(s).wait_recv()

    probe_out_ref[...] = sums[0]

    for k in range(waves):
        @pl.when(s < sections - 1)
        def _():
            copy_f(k).wait_send()

        @pl.when(s > 0)
        def _():
            copy_b(k).wait_send()


def shards(sections, tiles, slab, probe, amplitudes, offsets, counts):
    layers, _, side, _ = slab.shape
    n = probe.shape[-1]
    waves = offsets.shape[0] * 2
    lines = 4 * n // sections
    share = lines // tiles
    piece = (sections, n) if share == 1 else (sections, share, n)
    sum_rows = max(8, share)
    vmem = pl.BlockSpec(memory_space=pltpu.VMEM)
    smem = pl.BlockSpec(memory_space=pltpu.SMEM)
    wave = (waves, 2, n, n)
    grad, probe_grad = pl.pallas_call(
        functools.partial(kernel, sections, tiles),
        out_shape=(
            jax.ShapeDtypeStruct(slab.shape, F32),
            jax.ShapeDtypeStruct((sum_rows, n), F32),
        ),
        in_specs=[vmem, vmem, vmem, smem, smem, vmem],
        out_specs=(vmem, vmem),
        scratch_shapes=[
            pltpu.VMEM((side, side * layers * 4), BF16),
            pltpu.VMEM((waves // 2, layers, 2, n, n), F32),
            pltpu.VMEM((2, n, n), F32),
            pltpu.VMEM(wave, F32),
            pltpu.VMEM((2, 2, n, n), F32),
            pltpu.VMEM((2, 2, n, n), F32),
            pltpu.VMEM((layers, 2, n, n), F32),
            pltpu.VMEM((sections, lines, n), F32),
            pltpu.VMEM(wave, BF16),
            pltpu.VMEM(wave, BF16),
            pltpu.VMEM(wave, BF16),
            pltpu.VMEM(wave, BF16),
            pltpu.VMEM((tiles,) + piece, F32),
            pltpu.VMEM((sections, sum_rows, n), F32),
            pltpu.SemaphoreType.DMA((waves,)),
            pltpu.SemaphoreType.DMA((waves,)),
            pltpu.SemaphoreType.DMA((waves,)),
            pltpu.SemaphoreType.DMA((waves,)),
            pltpu.SemaphoreType.DMA((tiles,)),
            pltpu.SemaphoreType.DMA((tiles,)),
            pltpu.SemaphoreType.DMA((sections,)),
            pltpu.SemaphoreType.DMA,
        ],
        compiler_params=pltpu.CompilerParams(
            collective_id=0, has_side_effects=True, vmem_limit_bytes=48 * 1024 * 1024),
    )(slab, probe, amplitudes, offsets, counts, jnp.asarray(tables(n)))
    return grad, probe_grad[:share].reshape(-1)


def solution(mesh):
    body = functools.partial(shards, mesh.shape["sec"], mesh.shape["tile"])
    in_specs = (
        P("sec", None, "tile", None),
        P(),
        P("tile", None, None),
        P("tile", None),
        P("tile"),
    )
    out_specs = (P("sec", None, "tile", None), P(("sec", "tile")))
    return jax.shard_map(body, mesh=mesh, in_specs=in_specs, out_specs=out_specs, check_vma=False)
```

```python
import functools

import jax
import jax.numpy as jnp
import ml_dtypes
import numpy as np
from jax import lax
from jax.experimental import pallas as pl
from jax.experimental.pallas import tpu as pltpu
from jax.sharding import PartitionSpec as P

PHASE_SCALE = 20.0
F32 = jnp.float32
BF16 = jnp.bfloat16
MESH = pl.DeviceIdType.MESH


def real_forms(matrix):
    re, im = matrix.real, matrix.imag
    left = np.block([[re, -im], [im, re]])
    right = np.block([[re, im], [-im, re]])
    pieces = []
    for table in (right, left):
        table = table.astype(np.float32)
        high = table.astype(ml_dtypes.bfloat16)
        low = (table - high.astype(np.float32)).astype(ml_dtypes.bfloat16)
        pieces += [high, low]
    return pieces


def tables(length):
    index = np.arange(length)
    dft = np.exp(-2j * np.pi * (np.outer(index, index) % length) / length)
    frequency = np.where(index < (length + 1) // 2, index, index - length) / length
    phases = np.exp(-1j * PHASE_SCALE * frequency * frequency)
    propagator = (dft.conj() @ (phases[:, None] * dft)) / length
    return np.stack(real_forms(propagator) + real_forms(dft / np.sqrt(length)))


def split(value):
    high = value.astype(BF16)
    return high, (value - high.astype(F32)).astype(BF16)


def dot(a, b):
    return jnp.dot(a, b, preferred_element_type=F32)


def two_sided(tab_ref, right, left, re, im):
    n = re.shape[0]
    high, low = split(jnp.concatenate([re, im], axis=1))
    right_high = tab_ref[right]
    half = dot(high, right_high) + dot(low, right_high) + dot(high, tab_ref[right + 1])
    high, low = split(jnp.concatenate([half[:, :n], half[:, n:]], axis=0))
    both = dot(tab_ref[left], jnp.concatenate([high, low], axis=1))
    out = both[:, :n] + both[:, n:] + dot(tab_ref[left + 1], high)
    return out[:n], out[n:]


def one_hot(rows, columns, row_shift, column_shift):
    down = lax.broadcasted_iota(jnp.int32, (rows, columns), 0) + row_shift
    across = lax.broadcasted_iota(jnp.int32, (rows, columns), 1) + column_shift
    return jnp.where(down == across, 1.0, 0.0).astype(BF16)


def by_section(section, values):
    picked = values[0]
    for at in range(1, len(values)):
        if values[at] != values[at - 1]:
            picked = jnp.where(section >= at, values[at], picked)
    return picked


def kernel(
    sizes, tiles,
    slab_hbm, probe_hbm, amps_hbm, offsets_ref, counts_ref, tab_hbm,
    grad_ref, probe_out_ref,
    slab_ref, probe_ref, amps_ref, tab_ref,
    slab_parts, win, win_b, send_w, fields, cur, patch, send_g, recv_g, probe_acc,
    send_f, recv_f, send_b, recv_b, pieces, sums,
    sem_in, sem_sw, sem_rw, sem_sg, sem_rg, sem_sf, sem_rf, sem_sb, sem_rb, sem_ps, sem_pr, sem_zs, sem_zr, sem_go,
):
    n = probe_ref.shape[-1]
    side = slab_ref.shape[-1]
    slots = recv_g.shape[0]
    sections = sum(sizes)
    s = lax.axis_index("sec")
    t = lax.axis_index("tile")
    starts = [sum(sizes[:k]) for k in range(len(sizes))]
    group_of = [k for k, size in enumerate(sizes) for _ in range(size)]
    final = len(sizes) - 1
    size = by_section(s, [sizes[k] for k in group_of])
    start = by_section(s, [starts[k] for k in group_of])
    size_before = by_section(s, [sizes[max(k - 1, 0)] for k in group_of])
    start_before = by_section(s, [starts[max(k - 1, 0)] for k in group_of])
    size_after = by_section(s, [sizes[min(k + 1, final)] for k in group_of])
    start_after = by_section(s, [starts[min(k + 1, final)] for k in group_of])
    links_before = by_section(s, [max(1, sizes[max(k - 1, 0)] // sizes[k]) for k in group_of])
    links_after = by_section(s, [max(1, sizes[min(k + 1, final)] // sizes[k]) for k in group_of])
    rounds = by_section(s, [slots // sizes[k] for k in group_of])
    j = s - start
    first, last = s < starts[1], s >= starts[final]
    heads = sizes[0]

    inputs = [
        pltpu.make_async_copy(source, target, sem_in.at[at])
        for at, (source, target) in enumerate(
            ((slab_hbm, slab_ref), (tab_hbm, tab_ref), (probe_hbm, probe_ref), (amps_hbm, amps_ref)))
    ]
    for copy in inputs:
        copy.start()

    barrier = pltpu.get_barrier_semaphore()

    def greet(sec, tile):
        pl.semaphore_signal(barrier, inc=1, device_id=(sec, tile), device_id_type=MESH)

    for other in range(max(sizes)):
        @pl.when((other < size) & (other != j))
        def _():
            greet(start + other, t)

        @pl.when(jnp.logical_not(first) & (other < links_before))
        def _():
            greet(start_before + (j + size * other) % size_before, t)

        @pl.when(jnp.logical_not(last) & (other < links_after))
        def _():
            greet(start_after + (j + size * other) % size_after, t)

    near_zero = first | ((start == starts[1]) & (j % heads == 0))

    @pl.when(jnp.logical_not(near_zero))
    def _():
        greet(0, t)

    @pl.when(s == 0)
    def _():
        def greet_tile(step, carry):
            for member in range(heads):
                greet(member, (t + step) % tiles)
            return carry

        lax.fori_loop(1, tiles, greet_tile, 0)

    greetings = size - 1
    greetings += jnp.where(first, 0, links_before) + jnp.where(last, 0, links_after)
    greetings += jnp.where(first, tiles - 1, 0)
    greetings += jnp.where(s == 0, sections - heads - max(1, sizes[1] // heads), 0)

    grad_ref[...] = jnp.zeros_like(grad_ref)
    probe_acc[...] = jnp.zeros_like(probe_acc)

    planes = [(l, c) for l in range(2) for c in range(2)]
    inputs[0].wait()
    for at, (l, c) in enumerate(planes):
        high, low = split(slab_ref[l, c])
        slab_parts[:, at * side:(at + 1) * side] = high
        shift = (at + len(planes)) * side
        slab_parts[:, shift:shift + side] = low

    def cut(p, target):
        rows = one_hot(n, side, offsets_ref[p, 0], 0)
        columns = one_hot(side, n, 0, offsets_ref[p, 1])
        for at, (l, c) in enumerate(planes):
            value = None
            for part in (at, at + len(planes)):
                strip = dot(rows, slab_parts[:, part * side:(part + 1) * side]).astype(BF16)
                term = dot(strip, columns)
                value = term if value is None else value + term
            target[l, c] = value.astype(target.dtype)

    def place(p):
        rows = one_hot(side, n, 0, offsets_ref[p, 0])
        columns = one_hot(n, side, offsets_ref[p, 1], 0)
        for l, c in planes:
            strip = dot(recv_g[p, l, c], columns).astype(BF16)
            grad_ref[l, c] += dot(rows, strip)

    def copy_w(p):
        return pltpu.make_async_remote_copy(
            src_ref=send_w.at[p], dst_ref=win_b.at[(p // size) * size + j], send_sem=sem_sw.at[p],
            recv_sem=sem_rw.at[(p // size) * size + j], device_id=(start + p % size, t), device_id_type=MESH)

    def window_arrival(pair, owner):
        return pltpu.make_async_remote_copy(
            src_ref=send_w.at[0], dst_ref=win_b.at[pair], send_sem=sem_sw.at[0],
            recv_sem=sem_rw.at[pair], device_id=(start + owner, t), device_id_type=MESH)

    def copy_g(p, owner):
        pair = (p // size) * size + owner
        return pltpu.make_async_remote_copy(
            src_ref=send_g.at[pair], dst_ref=recv_g.at[p], send_sem=sem_sg.at[pair],
            recv_sem=sem_rg.at[p], device_id=(start + owner, t), device_id_type=MESH)

    def copy_f(p, m):
        return pltpu.make_async_remote_copy(
            src_ref=send_f.at[p, m], dst_ref=recv_f.at[p, m], send_sem=sem_sf.at[p, m], recv_sem=sem_rf.at[p, m],
            device_id=(start_after + p % size_after, t), device_id_type=MESH)

    def copy_b(p, m):
        return pltpu.make_async_remote_copy(
            src_ref=send_b.at[p, m], dst_ref=recv_b.at[p, m], send_sem=sem_sb.at[p, m], recv_sem=sem_rb.at[p, m],
            device_id=(start_before + p % size_before, t), device_id_type=MESH)

    def cut_round(i):
        def one(step, carry):
            member = (j + step) % size
            p = i * size + member

            @pl.when(step < size)
            def _():
                cut(p, send_w.at[p])
                copy_w(p).start()

            @pl.when(step == size)
            def _():
                cut(p, win.at[i * size + j])

            return carry

        lax.fori_loop(1, size + 1, one, 0)

    pl.semaphore_wait(barrier, greetings)
    cut_round(0)

    @pl.when(rounds > 1)
    def _():
        cut_round(1)

    for copy in inputs[1:]:
        copy.wait()

    def forward(i):
        p = i * size + j
        base = i * size * 2

        @pl.when(first)
        def _():
            for m in range(2):
                fields[base, m] = probe_ref[m]

        @pl.when(jnp.logical_not(first))
        def _():
            for m in range(2):
                copy_f(p, m).wait_recv()
                fields[base, m] = recv_f[p, m].astype(F32)

        def slices(owner, carry):
            @pl.when(owner != j)
            def _():
                pair = i * size + owner
                window_arrival(pair, owner).wait_recv()
                win[pair] = win_b[pair].astype(F32)

            for half in range(2):
                at = base + 2 * owner + half
                tr, ti = win[i * size + owner, half, 0], win[i * size + owner, half, 1]
                results = []
                for m in range(2):
                    re, im = fields[at, m, 0], fields[at, m, 1]
                    results.append(two_sided(tab_ref, 0, 2, tr * re - ti * im, tr * im + ti * re))
                for m in range(2):
                    fields[at + 1, m, 0], fields[at + 1, m, 1] = results[m]
            return carry

        lax.fori_loop(0, size, slices, 0)
        end = base + 2 * size

        @pl.when(jnp.logical_not(last))
        def _():
            for m in range(2):
                send_f[p, m] = fields[end, m].astype(BF16)
                copy_f(p, m).start()

        @pl.when(last)
        def _():
            far(p, end)

    def far(p, end):
        spectrum = [two_sided(tab_ref, 4, 6, fields[end, m, 0], fields[end, m, 1]) for m in range(2)]
        intensity = sum(re * re + im * im for re, im in spectrum)
        modelled = jnp.sqrt(intensity + 0.25)
        live = jnp.where(p < counts_ref[0], 2.0, 0.0)
        factor = live * (1.0 - amps_ref[p].astype(F32) / modelled)
        for m, (re, im) in enumerate(spectrum):
            cur[m, 0], cur[m, 1] = two_sided(tab_ref, 6, 4, factor * re, factor * im)

    def backward(i):
        p = i * size + j
        base = i * size * 2

        @pl.when(jnp.logical_not(last))
        def _():
            for m in range(2):
                copy_b(p, m).wait_recv()
                cur[m] = recv_b[p, m].astype(F32)

        def slices(step, carry):
            owner = size - 1 - step
            for half in (1, 0):
                at = base + 2 * owner + half
                tr, ti = win[i * size + owner, half, 0], win[i * size + owner, half, 1]
                middle = [two_sided(tab_ref, 2, 0, cur[m, 0], cur[m, 1]) for m in range(2)]
                piece_re = piece_im = 0.0
                for m, (re, im) in enumerate(middle):
                    xr, xi = fields[at, m, 0], fields[at, m, 1]
                    piece_re += xr * re + xi * im
                    piece_im += xr * im - xi * re
                    cur[m, 0] = tr * re + ti * im
                    cur[m, 1] = tr * im - ti * re
                patch[half, 0] = piece_re.astype(BF16)
                patch[half, 1] = piece_im.astype(BF16)

            @pl.when(owner == j)
            def _():
                recv_g[p] = patch[...]

            @pl.when(owner != j)
            def _():
                send_g[i * size + owner] = patch[...]

                @pl.when(first)
                def _():
                    copy_g(p, owner).start()

            return carry

        lax.fori_loop(0, size, slices, 0)

        @pl.when(jnp.logical_not(first))
        def _():
            for m in range(2):
                send_b[p, m] = cur[m].astype(BF16)
                copy_b(p, m).start()

        @pl.when(first)
        def _():
            groups = sections // 4
            for m in range(2):
                for c in range(2):
                    where = pl.ds((2 * m + c) * groups, groups)
                    probe_acc[where] += cur[m, c].reshape((groups,) + probe_acc.shape[1:])

    def send_patches():
        @pl.when(j == size - 1)
        def _():
            for m in range(2):
                copy_b((rounds - 1) * size + j, m).wait_send()

            def allow(step, carry):
                pl.semaphore_signal(sem_go, inc=1, device_id=(start + step, t), device_id_type=MESH)
                return carry

            lax.fori_loop(0, size - 1, allow, 0)

        @pl.when(j < size - 1)
        def _():
            pl.semaphore_wait(sem_go, 1)

        def of_round(i, carry):
            def one(step, inner):
                copy_g(i * size + j, (j + step) % size).start()
                return inner

            return lax.fori_loop(1, size, one, carry)

        lax.fori_loop(0, rounds, of_round, 0)

    def place_round(i):
        def one(step, carry):
            member = (j + step) % size
            p = i * size + member

            @pl.when(step > 0)
            def _():
                pltpu.make_async_remote_copy(
                    src_ref=send_g.at[0], dst_ref=recv_g.at[p], send_sem=sem_sg.at[0],
                    recv_sem=sem_rg.at[p], device_id=(start + member, t), device_id_type=MESH).wait_recv()

            place(p)
            return carry

        lax.fori_loop(0, size, one, 0)

    def turn(u, carry):
        onward = jnp.where(last, u % 2 == 0, u < rounds)

        @pl.when(onward)
        def _():
            i = jnp.where(last, u // 2, u)
            forward(i)

            @pl.when(i + 2 < rounds)
            def _():
                cut_round(i + 2)

        @pl.when(jnp.logical_not(onward))
        def _():
            i = jnp.where(last, u // 2, u - rounds)
            backward(i)

            @pl.when(first & (i > 0))
            def _():
                place_round(i - 1)

        return carry

    lax.fori_loop(0, 2 * rounds, turn, 0)

    share = probe_acc.shape[1] // tiles

    def of_tile(other):
        return probe_acc.at[:, other] if share == 1 else probe_acc.at[:, pl.ds(other * share, share)]

    def copy_p(other):
        return pltpu.make_async_remote_copy(
            src_ref=of_tile(other), dst_ref=pieces.at[j * tiles + t], send_sem=sem_ps.at[other],
            recv_sem=sem_pr.at[j * tiles + t], device_id=(0, other), device_id_type=MESH)

    def arrival_p(slot):
        return pltpu.make_async_remote_copy(
            src_ref=of_tile(0), dst_ref=pieces.at[slot], send_sem=sem_ps.at[0], recv_sem=sem_pr.at[slot],
            device_id=(0, t), device_id_type=MESH)

    def copy_z(sec):
        return pltpu.make_async_remote_copy(
            src_ref=sums.at[sec], dst_ref=sums.at[0], send_sem=sem_zs.at[sec], recv_sem=sem_zr,
            device_id=(sec, t), device_id_type=MESH)

    @pl.when(first)
    def _():
        for other in range(tiles):
            @pl.when((other != t) | (j > 0))
            def _():
                copy_p(other).start()

            @pl.when((other == t) & (j == 0))
            def _():
                pieces[other] = of_tile(other)[...]

    @pl.when(first)
    def _():
        place_round(rounds - 1)

    @pl.when(jnp.logical_not(first))
    def _():
        send_patches()

        def placing(i, carry):
            place_round(i)
            return carry

        lax.fori_loop(0, rounds, placing, 0)

    @pl.when(s == 0)
    def _():
        def arrive(slot, carry):
            @pl.when(slot != t)
            def _():
                arrival_p(slot).wait_recv()

            return carry

        lax.fori_loop(0, heads * tiles, arrive, 0)
        total = pieces[0]
        for slot in range(1, heads * tiles):
            total = total + pieces[slot]
        for sec in range(sections):
            sums[sec] = jnp.broadcast_to(total[sec], sums.shape[1:])
        for sec in range(1, sections):
            copy_z(sec).start()
        for sec in range(1, sections):
            copy_z(sec).wait_send()

    @pl.when(s > 0)
    def _():
        copy_z(s).wait_recv()

    probe_out_ref[...] = sums[0]

    @pl.when(first)
    def _():
        for other in range(tiles):
            @pl.when((other != t) | (j > 0))
            def _():
                copy_p(other).wait_send()

    def sent(p, carry):
        @pl.when(p % size != j)
        def _():
            copy_w(p).wait_send()

        @pl.when(p % size == j)
        def _():
            for m in range(2):
                @pl.when(jnp.logical_not(last))
                def _():
                    copy_f(p, m).wait_send()

                @pl.when(jnp.logical_not(first) & ((j < size - 1) | (p < slots - 1)))
                def _():
                    copy_b(p, m).wait_send()

            def sent_piece(owner, inner):
                @pl.when(owner != j)
                def _():
                    copy_g(p, owner).wait_send()

                return inner

            lax.fori_loop(0, size, sent_piece, 0)

        return carry

    lax.fori_loop(0, slots, sent, 0)


GROUPS = {16: (2, 2, 4, 8), 8: (2, 2, 4), 4: (2, 2)}


def shards(sections, tiles, slab, probe, amplitudes, offsets, counts):
    layers, _, side, _ = slab.shape
    n = probe.shape[-1]
    slots = offsets.shape[0]
    sizes = GROUPS[sections]
    lines = 4 * n // sections
    share = lines // tiles
    piece = (sections, n) if share == 1 else (sections, share, n)
    sum_rows = max(8, share)
    hbm = pl.BlockSpec(memory_space=pl.ANY)
    vmem = pl.BlockSpec(memory_space=pltpu.VMEM)
    smem = pl.BlockSpec(memory_space=pltpu.SMEM)
    tab = jnp.asarray(tables(n))
    window = (layers, 2, n, n)
    wave = (slots, 2, 2, n, n)
    dma = pltpu.SemaphoreType.DMA
    grad, probe_grad = pl.pallas_call(
        functools.partial(kernel, sizes, tiles),
        out_shape=(
            jax.ShapeDtypeStruct(slab.shape, F32),
            jax.ShapeDtypeStruct((sum_rows, n), F32),
        ),
        in_specs=[hbm, hbm, hbm, smem, smem, hbm],
        out_specs=(vmem, vmem),
        scratch_shapes=[
            pltpu.VMEM(slab.shape, F32),
            pltpu.VMEM(probe.shape, F32),
            pltpu.VMEM(amplitudes.shape, BF16),
            pltpu.VMEM(tab.shape, BF16),
            pltpu.VMEM((side, side * layers * 4), BF16),
            pltpu.VMEM((slots,) + window, F32),
            pltpu.VMEM((slots,) + window, BF16),
            pltpu.VMEM((slots,) + window, BF16),
            pltpu.VMEM((slots * layers + 1, 2, 2, n, n), F32),
            pltpu.VMEM((2, 2, n, n), F32),
            pltpu.VMEM(window, BF16),
            pltpu.VMEM((slots,) + window, BF16),
            pltpu.VMEM((slots,) + window, BF16),
            pltpu.VMEM((sections, lines, n), F32),
            pltpu.VMEM(wave, BF16),
            pltpu.VMEM(wave, BF16),
            pltpu.VMEM(wave, BF16),
            pltpu.VMEM(wave, BF16),
            pltpu.VMEM((sizes[0] * tiles,) + piece, F32),
            pltpu.VMEM((sections, sum_rows, n), F32),
            dma((4,)),
            dma((slots,)), dma((slots,)),
            dma((slots,)), dma((slots,)),
            dma((slots, 2)), dma((slots, 2)),
            dma((slots, 2)), dma((slots, 2)),
            dma((tiles,)), dma((sizes[0] * tiles,)),
            dma((sections,)), dma,
            pltpu.SemaphoreType.REGULAR,
        ],
        compiler_params=pltpu.CompilerParams(
            collective_id=0, has_side_effects=True, vmem_limit_bytes=56 * 1024 * 1024),
    )(slab, probe, amplitudes, offsets, counts, tab)
    return grad, probe_grad[:share].reshape(-1)


def solution(mesh):
    body = functools.partial(shards, mesh.shape["sec"], mesh.shape["tile"])
    in_specs = (
        P("sec", None, "tile", None),
        P(),
        P("tile", None, None),
        P("tile", None),
        P("tile"),
    )
    out_specs = (P("sec", None, "tile", None), P(("sec", "tile")))
    return jax.shard_map(body, mesh=mesh, in_specs=in_specs, out_specs=out_specs, check_vma=False)
```

```python
import functools

import jax
import jax.numpy as jnp
import ml_dtypes
import numpy as np
from jax import lax
from jax.experimental import pallas as pl
from jax.experimental.pallas import tpu as pltpu
from jax.sharding import PartitionSpec as P

PHASE_SCALE = 20.0
F32 = jnp.float32
BF16 = jnp.bfloat16
MESH = pl.DeviceIdType.MESH


def real_forms(matrix):
    re, im = matrix.real, matrix.imag
    left = np.block([[re, -im], [im, re]])
    right = np.block([[re, im], [-im, re]])
    pieces = []
    for table in (right, left):
        table = table.astype(np.float32)
        high = table.astype(ml_dtypes.bfloat16)
        low = (table - high.astype(np.float32)).astype(ml_dtypes.bfloat16)
        pieces += [high, low]
    return pieces


def tables(length):
    index = np.arange(length)
    dft = np.exp(-2j * np.pi * (np.outer(index, index) % length) / length)
    frequency = np.where(index < (length + 1) // 2, index, index - length) / length
    phases = np.exp(-1j * PHASE_SCALE * frequency * frequency)
    propagator = (dft.conj() @ (phases[:, None] * dft)) / length
    return np.stack(real_forms(propagator) + real_forms(dft / np.sqrt(length)))


def split(value):
    high = value.astype(BF16)
    return high, (value - high.astype(F32)).astype(BF16)


def dot(a, b):
    return jnp.dot(a, b, preferred_element_type=F32)


def two_sided(tab_ref, right, left, re, im):
    n = re.shape[0]
    high, low = split(jnp.concatenate([re, im], axis=1))
    right_high = tab_ref[right]
    half = dot(high, right_high) + dot(low, right_high) + dot(high, tab_ref[right + 1])
    high, low = split(jnp.concatenate([half[:, :n], half[:, n:]], axis=0))
    both = dot(tab_ref[left], jnp.concatenate([high, low], axis=1))
    out = both[:, :n] + both[:, n:] + dot(tab_ref[left + 1], high)
    return out[:n], out[n:]


def one_hot(rows, columns, row_shift, column_shift):
    down = lax.broadcasted_iota(jnp.int32, (rows, columns), 0) + row_shift
    across = lax.broadcasted_iota(jnp.int32, (rows, columns), 1) + column_shift
    return jnp.where(down == across, 1.0, 0.0).astype(BF16)


def by_section(section, values):
    picked = values[0]
    for at in range(1, len(values)):
        if values[at] != values[at - 1]:
            picked = jnp.where(section >= at, values[at], picked)
    return picked


def kernel(
    sizes, tiles,
    slab_hbm, probe_hbm, amps_hbm, offsets_ref, counts_ref, tab_hbm,
    grad_ref, probe_out_ref,
    slab_ref, probe_ref, amps_ref, tab_ref,
    slab_parts, win, win_b, send_w, fields, cur, patch, send_g, recv_g, probe_acc, stage,
    send_f, recv_f, send_b, recv_b, pieces, sums, own_sum,
    sem_in, sem_sw, sem_rw, sem_sg, sem_rg, sem_sf, sem_rf, sem_sb, sem_rb, sem_ps, sem_pr, sem_zs, sem_zr, sem_go,
):
    n = probe_ref.shape[-1]
    side = slab_ref.shape[-1]
    slots = recv_g.shape[0]
    sections = sum(sizes)
    s = lax.axis_index("sec")
    t = lax.axis_index("tile")
    starts = [sum(sizes[:k]) for k in range(len(sizes))]
    group_of = [k for k, size in enumerate(sizes) for _ in range(size)]
    final = len(sizes) - 1
    size = by_section(s, [sizes[k] for k in group_of])
    start = by_section(s, [starts[k] for k in group_of])
    size_before = by_section(s, [sizes[max(k - 1, 0)] for k in group_of])
    start_before = by_section(s, [starts[max(k - 1, 0)] for k in group_of])
    size_after = by_section(s, [sizes[min(k + 1, final)] for k in group_of])
    start_after = by_section(s, [starts[min(k + 1, final)] for k in group_of])
    links_before = by_section(s, [max(1, sizes[max(k - 1, 0)] // sizes[k]) for k in group_of])
    links_after = by_section(s, [max(1, sizes[min(k + 1, final)] // sizes[k]) for k in group_of])
    rounds = by_section(s, [slots // sizes[k] for k in group_of])
    j = s - start
    first, last = s < starts[1], s >= starts[final]
    heads = sizes[0]

    inputs = [
        pltpu.make_async_copy(source, target, sem_in.at[at])
        for at, (source, target) in enumerate(
            ((slab_hbm, slab_ref), (tab_hbm, tab_ref), (probe_hbm, probe_ref), (amps_hbm, amps_ref)))
    ]
    for copy in inputs:
        copy.start()

    barrier = pltpu.get_barrier_semaphore()

    def greet(sec, tile):
        pl.semaphore_signal(barrier, inc=1, device_id=(sec, tile), device_id_type=MESH)

    for other in range(max(sizes)):
        @pl.when((other < size) & (other != j))
        def _():
            greet(start + other, t)

        @pl.when(jnp.logical_not(first) & (other < links_before))
        def _():
            greet(start_before + (j + size * other) % size_before, t)

        @pl.when(jnp.logical_not(last) & (other < links_after))
        def _():
            greet(start_after + (j + size * other) % size_after, t)

    per = sections // heads
    strangers = [
        int(k > 0 and not (k == 1 and (x - starts[1]) % heads == x // per)) for x, k in enumerate(group_of)]
    from_strangers = [sum(strangers[x * per:(x + 1) * per]) if x < heads else 0 for x in range(sections)]
    summer = s // per

    @pl.when(by_section(s, strangers) == 1)
    def _():
        greet(summer, t)

    @pl.when(first)
    def _():
        def greet_tile(step, carry):
            for member in range(heads):
                greet(member, (t + step) % tiles)
            return carry

        lax.fori_loop(1, tiles, greet_tile, 0)

    greetings = size - 1
    greetings += jnp.where(first, 0, links_before) + jnp.where(last, 0, links_after)
    greetings += jnp.where(first, (tiles - 1) * heads, 0) + by_section(s, from_strangers)

    grad_ref[...] = jnp.zeros_like(grad_ref)
    probe_acc[...] = jnp.zeros_like(probe_acc)

    planes = [(l, c) for l in range(2) for c in range(2)]
    inputs[0].wait()
    for at, (l, c) in enumerate(planes):
        high, low = split(slab_ref[l, c])
        slab_parts[:, at * side:(at + 1) * side] = high
        shift = (at + len(planes)) * side
        slab_parts[:, shift:shift + side] = low

    def cut(p, target, parts):
        rows = one_hot(n, side, offsets_ref[p, 0], 0)
        columns = one_hot(side, n, 0, offsets_ref[p, 1])
        for at, (l, c) in enumerate(planes):
            value = None
            for part in range(at, at + parts * len(planes), len(planes)):
                strip = dot(rows, slab_parts[:, part * side:(part + 1) * side]).astype(BF16)
                term = dot(strip, columns)
                value = term if value is None else value + term
            target[l, c] = value.astype(target.dtype)

    def place(p):
        rows = one_hot(side, n, 0, offsets_ref[p, 0])
        columns = one_hot(n, side, offsets_ref[p, 1], 0)
        for l, c in planes:
            strip = dot(recv_g[p, l, c], columns).astype(BF16)
            grad_ref[l, c] += dot(rows, strip)

    def copy_w(p):
        return pltpu.make_async_remote_copy(
            src_ref=send_w.at[p], dst_ref=win_b.at[(p // size) * size + j], send_sem=sem_sw.at[p],
            recv_sem=sem_rw.at[(p // size) * size + j], device_id=(start + p % size, t), device_id_type=MESH)

    def window_arrival(pair, owner):
        return pltpu.make_async_remote_copy(
            src_ref=send_w.at[0], dst_ref=win_b.at[pair], send_sem=sem_sw.at[0],
            recv_sem=sem_rw.at[pair], device_id=(start + owner, t), device_id_type=MESH)

    def copy_g(p, owner):
        pair = (p // size) * size + owner
        return pltpu.make_async_remote_copy(
            src_ref=send_g.at[pair], dst_ref=recv_g.at[p], send_sem=sem_sg.at[pair],
            recv_sem=sem_rg.at[p], device_id=(start + owner, t), device_id_type=MESH)

    def copy_f(p, m):
        return pltpu.make_async_remote_copy(
            src_ref=send_f.at[p, m], dst_ref=recv_f.at[p, m], send_sem=sem_sf.at[p, m], recv_sem=sem_rf.at[p, m],
            device_id=(start_after + p % size_after, t), device_id_type=MESH)

    def copy_b(p, m):
        return pltpu.make_async_remote_copy(
            src_ref=send_b.at[p, m], dst_ref=recv_b.at[p, m], send_sem=sem_sb.at[p, m], recv_sem=sem_rb.at[p, m],
            device_id=(start_before + p % size_before, t), device_id_type=MESH)

    def cut_round(i):
        def one(step, carry):
            member = (j + step) % size
            p = i * size + member

            @pl.when(step < size)
            def _():
                cut(p, send_w.at[p], 1)
                copy_w(p).start()

            @pl.when(step == size)
            def _():
                cut(p, win.at[i * size + j], 2)

            return carry

        lax.fori_loop(1, size + 1, one, 0)

    pl.semaphore_wait(barrier, greetings)
    cut_round(0)

    def cut_ahead(i, carry):
        cut_round(i)
        return carry

    lax.fori_loop(1, jnp.where(first, jnp.minimum(rounds, 2), rounds), cut_ahead, 0)

    for copy in inputs[1:]:
        copy.wait()

    def forward(i, modes):
        fresh = True if len(modes) == 2 else modes[0] == 0
        p = i * size + j
        base = i * size * 2

        @pl.when(first)
        def _():
            for m in modes:
                fields[base, m] = probe_ref[m]

        @pl.when(jnp.logical_not(first))
        def _():
            for m in modes:
                copy_f(p, m).wait_recv()
                fields[base, m] = recv_f[p, m].astype(F32)

        def slices(owner, carry):
            @pl.when((owner != j) & fresh)
            def _():
                pair = i * size + owner
                window_arrival(pair, owner).wait_recv()
                win[pair] = win_b[pair].astype(F32)

            for half in range(2):
                at = base + 2 * owner + half
                tr, ti = win[i * size + owner, half, 0], win[i * size + owner, half, 1]
                results = []
                for m in modes:
                    re, im = fields[at, m, 0], fields[at, m, 1]
                    results.append(two_sided(tab_ref, 0, 2, tr * re - ti * im, tr * im + ti * re))
                for m, result in zip(modes, results):
                    fields[at + 1, m, 0], fields[at + 1, m, 1] = result
            return carry

        lax.fori_loop(0, size, slices, 0)
        end = base + 2 * size

        @pl.when(jnp.logical_not(last))
        def _():
            for m in modes:
                send_f[p, m] = fields[end, m].astype(BF16)
                copy_f(p, m).start()

        if len(modes) == 2:
            @pl.when(last)
            def _():
                far(p, end)

    def far(p, end):
        spectrum = [two_sided(tab_ref, 4, 6, fields[end, m, 0], fields[end, m, 1]) for m in range(2)]
        intensity = sum(re * re + im * im for re, im in spectrum)
        modelled = jnp.sqrt(intensity + 0.25)
        live = jnp.where(p < counts_ref[0], 2.0, 0.0)
        factor = live * (1.0 - amps_ref[p].astype(F32) / modelled)
        for m, (re, im) in enumerate(spectrum):
            cur[m, 0], cur[m, 1] = two_sided(tab_ref, 6, 4, factor * re, factor * im)

    def backward(i, modes):
        whole = True if len(modes) == 2 else modes[0] == 1
        p = i * size + j
        base = i * size * 2

        @pl.when(jnp.logical_not(last))
        def _():
            for m in modes:
                copy_b(p, m).wait_recv()
                cur[m] = recv_b[p, m].astype(F32)

        def slices(step, carry):
            owner = size - 1 - step
            for half in (1, 0):
                at = base + 2 * owner + half
                tr, ti = win[i * size + owner, half, 0], win[i * size + owner, half, 1]
                middle = [two_sided(tab_ref, 2, 0, cur[m, 0], cur[m, 1]) for m in modes]
                piece_re = piece_im = 0.0
                for m, (re, im) in zip(modes, middle):
                    xr, xi = fields[at, m, 0], fields[at, m, 1]
                    piece_re += xr * re + xi * im
                    piece_im += xr * im - xi * re
                    cur[m, 0] = tr * re + ti * im
                    cur[m, 1] = tr * im - ti * re
                piece = (piece_re, piece_im)
                if len(modes) == 2:
                    patch[half, 0], patch[half, 1] = [part.astype(BF16) for part in piece]
                else:
                    @pl.when(modes[0] == 0)
                    def _():
                        for c in range(2):
                            fields[at, 0, c] = piece[c]

                    @pl.when(modes[0] == 1)
                    def _():
                        for c in range(2):
                            patch[half, c] = (fields[at, 0, c] + piece[c]).astype(BF16)

            @pl.when((owner == j) & whole)
            def _():
                recv_g[p] = patch[...]

            @pl.when((owner != j) & whole)
            def _():
                send_g[i * size + owner] = patch[...]

                @pl.when(first)
                def _():
                    copy_g(p, owner).start()

            return carry

        lax.fori_loop(0, size, slices, 0)

        @pl.when(jnp.logical_not(first))
        def _():
            for m in modes:
                send_b[p, m] = cur[m].astype(BF16)
                copy_b(p, m).start()

        @pl.when(first)
        def _():
            for m in modes:
                for c in range(2):
                    probe_acc[pl.ds(pl.multiple_of((2 * m + c) * n, n), n)] += cur[m, c]

    def send_patches():
        @pl.when(j == size - 1)
        def _():
            for m in range(2):
                copy_b((rounds - 1) * size + j, m).wait_send()

            def allow(step, carry):
                pl.semaphore_signal(
                    sem_go, inc=1, device_id=(start + (j + step) % size, t), device_id_type=MESH)
                return carry

            lax.fori_loop(1, size, allow, 0)

        @pl.when(j < size - 1)
        def _():
            pl.semaphore_wait(sem_go, 1)

        def of_round(i, carry):
            def one(step, inner):
                copy_g(i * size + j, (j + step) % size).start()
                return inner

            return lax.fori_loop(1, size, one, carry)

        lax.fori_loop(0, rounds, of_round, 0)

    def place_round(i):
        def one(step, carry):
            member = (j + step) % size
            p = i * size + member

            @pl.when(step > 0)
            def _():
                pltpu.make_async_remote_copy(
                    src_ref=send_g.at[0], dst_ref=recv_g.at[p], send_sem=sem_sg.at[0],
                    recv_sem=sem_rg.at[p], device_id=(start + member, t), device_id_type=MESH).wait_recv()

            place(p)
            return carry

        lax.fori_loop(0, size, one, 0)

    alone = (size <= ALONE) & jnp.logical_not(last)

    def by_modes(work, i):
        @pl.when(alone)
        def _():
            def one(m, carry):
                work(i, (m,))
                return carry

            lax.fori_loop(0, 2, one, 0)

        @pl.when(jnp.logical_not(alone))
        def _():
            work(i, (0, 1))

    def turn(u, carry):
        onward = jnp.where(last, u % 2 == 0, u < rounds)

        @pl.when(onward)
        def _():
            i = jnp.where(last, u // 2, u)
            by_modes(forward, i)

            @pl.when(first & (i + 2 < rounds))
            def _():
                cut_round(i + 2)

        @pl.when(jnp.logical_not(onward))
        def _():
            i = jnp.where(last, u // 2, u - rounds)
            by_modes(backward, i)

        return carry

    lax.fori_loop(0, 2 * rounds, turn, 0)

    lines = 4 * n // sections
    share = lines // tiles

    def copy_p(member, other):
        return pltpu.make_async_remote_copy(
            src_ref=stage.at[other, :, pl.ds(member * per, per)], dst_ref=pieces.at[j * tiles + t],
            send_sem=sem_ps.at[member * tiles + other], recv_sem=sem_pr.at[j * tiles + t],
            device_id=(member, other), device_id_type=MESH)

    def arrival_p(slot):
        return pltpu.make_async_remote_copy(
            src_ref=stage.at[0, :, pl.ds(0, per)], dst_ref=pieces.at[slot], send_sem=sem_ps.at[0],
            recv_sem=sem_pr.at[slot], device_id=(s, t), device_id_type=MESH)

    def copy_z(at):
        return pltpu.make_async_remote_copy(
            src_ref=sums.at[at], dst_ref=own_sum, send_sem=sem_zs.at[at], recv_sem=sem_zr,
            device_id=(j * per + at, t), device_id_type=MESH)

    def each_piece(act):
        def one(step, carry):
            other = (t + step) % tiles
            for member in range(heads):
                @pl.when((step > 0) | (member != j))
                def _():
                    act(copy_p(member, other))

            return carry

        lax.fori_loop(0, tiles, one, 0)

    @pl.when(first)
    def _():
        for other in range(tiles):
            for k in range(share):
                stage[other, k] = probe_acc[pl.ds(other * share + k, sections, stride=lines), :]
        each_piece(lambda copy: copy.start())
        pieces[j * tiles + t] = stage[t, :, pl.ds(j * per, per)]

    @pl.when(jnp.logical_not(first))
    def _():
        send_patches()

    def placing(i, carry):
        place_round(i)
        return carry

    lax.fori_loop(0, rounds, placing, 0)

    @pl.when(first)
    def _():
        def arrive(slot, carry):
            @pl.when(slot != j * tiles + t)
            def _():
                arrival_p(slot).wait_recv()

            return carry

        lax.fori_loop(0, heads * tiles, arrive, 0)
        total = pieces[0]
        for slot in range(1, heads * tiles):
            total = total + pieces[slot]
        for at in range(per):
            sums[at] = jnp.broadcast_to(total[:, at], sums.shape[1:])
        for at in range(per):
            @pl.when(j * per + at != s)
            def _():
                copy_z(at).start()

            @pl.when(j * per + at == s)
            def _():
                own_sum[...] = sums[at]

    @pl.when(summer != s)
    def _():
        pltpu.make_async_remote_copy(
            src_ref=sums.at[0], dst_ref=own_sum, send_sem=sem_zs.at[0], recv_sem=sem_zr,
            device_id=(summer, t), device_id_type=MESH).wait_recv()

    probe_out_ref[...] = own_sum[0:share]

    @pl.when(first)
    def _():
        each_piece(lambda copy: copy.wait_send())
        for at in range(per):
            @pl.when(j * per + at != s)
            def _():
                copy_z(at).wait_send()

    def sent(p, carry):
        @pl.when(p % size != j)
        def _():
            copy_w(p).wait_send()

        @pl.when(p % size == j)
        def _():
            for m in range(2):
                @pl.when(jnp.logical_not(last))
                def _():
                    copy_f(p, m).wait_send()

                @pl.when(jnp.logical_not(first) & ((j < size - 1) | (p < slots - 1)))
                def _():
                    copy_b(p, m).wait_send()

            def sent_piece(owner, inner):
                @pl.when(owner != j)
                def _():
                    copy_g(p, owner).wait_send()

                return inner

            lax.fori_loop(0, size, sent_piece, 0)

        return carry

    lax.fori_loop(0, slots, sent, 0)


ALONE = 2
GROUPS = {16: (2, 2, 4, 8), 8: (2, 2, 4), 4: (2, 2)}


def shards(sections, tiles, slab, probe, amplitudes, offsets, counts):
    layers, _, side, _ = slab.shape
    n = probe.shape[-1]
    slots = offsets.shape[0]
    sizes = GROUPS[sections]
    lines = 4 * n // sections
    share = lines // tiles
    per = sections // sizes[0]
    sum_rows = max(8, share)
    hbm = pl.BlockSpec(memory_space=pltpu.HBM)
    vmem = pl.BlockSpec(memory_space=pltpu.VMEM)
    smem = pl.BlockSpec(memory_space=pltpu.SMEM)
    tab = jnp.asarray(tables(n))
    window = (layers, 2, n, n)
    wave = (slots, 2, 2, n, n)
    dma = pltpu.SemaphoreType.DMA
    grad, probe_grad = pl.pallas_call(
        functools.partial(kernel, sizes, tiles),
        out_shape=(
            jax.ShapeDtypeStruct(slab.shape, F32),
            jax.ShapeDtypeStruct((share, n), F32),
        ),
        in_specs=[hbm, hbm, hbm, smem, smem, hbm],
        out_specs=(vmem, vmem),
        scratch_shapes=[
            pltpu.VMEM(slab.shape, F32),
            pltpu.VMEM(probe.shape, F32),
            pltpu.VMEM(amplitudes.shape, BF16),
            pltpu.VMEM(tab.shape, BF16),
            pltpu.VMEM((side, side * layers * 4), BF16),
            pltpu.VMEM((slots,) + window, F32),
            pltpu.VMEM((slots,) + window, BF16),
            pltpu.VMEM((slots,) + window, BF16),
            pltpu.VMEM((slots * layers + 1, 2, 2, n, n), F32),
            pltpu.VMEM((2, 2, n, n), F32),
            pltpu.VMEM(window, BF16),
            pltpu.VMEM((slots,) + window, BF16),
            pltpu.VMEM((slots,) + window, BF16),
            pltpu.VMEM((4 * n, n), F32),
            pltpu.VMEM((tiles, share, sections, n), F32),
            pltpu.VMEM(wave, BF16),
            pltpu.VMEM(wave, BF16),
            pltpu.VMEM(wave, BF16),
            pltpu.VMEM(wave, BF16),
            pltpu.VMEM((sizes[0] * tiles, share, per, n), F32),
            pltpu.VMEM((per, sum_rows, n), F32),
            pltpu.VMEM((sum_rows, n), F32),
            dma((4,)),
            dma((slots,)), dma((slots,)),
            dma((slots,)), dma((slots,)),
            dma((slots, 2)), dma((slots, 2)),
            dma((slots, 2)), dma((slots, 2)),
            dma((sizes[0] * tiles,)), dma((sizes[0] * tiles,)),
            dma((per,)), dma,
            pltpu.SemaphoreType.REGULAR,
        ],
        compiler_params=pltpu.CompilerParams(
            collective_id=0, has_side_effects=True, vmem_limit_bytes=56 * 1024 * 1024),
    )(slab, probe, amplitudes, offsets, counts, tab)
    return grad, probe_grad.reshape(-1)


def solution(mesh):
    body = functools.partial(shards, mesh.shape["sec"], mesh.shape["tile"])
    in_specs = (
        P("sec", None, "tile", None),
        P(),
        P("tile", None, None),
        P("tile", None),
        P("tile"),
    )
    out_specs = (P("sec", None, "tile", None), P(("sec", "tile")))
    return jax.shard_map(body, mesh=mesh, in_specs=in_specs, out_specs=out_specs, check_vma=False)
```

```python
import functools

import jax
import jax.numpy as jnp
import ml_dtypes
import numpy as np
from jax import lax
from jax.experimental import pallas as pl
from jax.experimental.pallas import tpu as pltpu
from jax.sharding import PartitionSpec as P

PHASE_SCALE = 20.0
F32 = jnp.float32
BF16 = jnp.bfloat16
MESH = pl.DeviceIdType.MESH


def real_forms(matrix):
    re, im = matrix.real, matrix.imag
    left = np.block([[re, -im], [im, re]])
    right = np.block([[re, im], [-im, re]])
    pieces = []
    for table in (right, left):
        table = table.astype(np.float32)
        high = table.astype(ml_dtypes.bfloat16)
        low = (table - high.astype(np.float32)).astype(ml_dtypes.bfloat16)
        pieces += [high, low]
    return pieces


def tables(length):
    index = np.arange(length)
    dft = np.exp(-2j * np.pi * (np.outer(index, index) % length) / length)
    frequency = np.where(index < (length + 1) // 2, index, index - length) / length
    phases = np.exp(-1j * PHASE_SCALE * frequency * frequency)
    propagator = (dft.conj() @ (phases[:, None] * dft)) / length
    return np.stack(real_forms(propagator) + real_forms(dft / np.sqrt(length)))


def split(value):
    high = value.astype(BF16)
    return high, (value - high.astype(F32)).astype(BF16)


def dot(a, b):
    return jnp.dot(a, b, preferred_element_type=F32)


def two_sided(tab_ref, right, left, re, im):
    n = re.shape[0]
    high, low = split(jnp.concatenate([re, im], axis=1))
    right_high = tab_ref[right]
    half = dot(high, right_high) + dot(low, right_high) + dot(high, tab_ref[right + 1])
    high, low = split(jnp.concatenate([half[:, :n], half[:, n:]], axis=0))
    both = dot(tab_ref[left], jnp.concatenate([high, low], axis=1))
    out = both[:, :n] + both[:, n:] + dot(tab_ref[left + 1], high)
    return out[:n], out[n:]


def one_hot(rows, columns, row_shift, column_shift):
    down = lax.broadcasted_iota(jnp.int32, (rows, columns), 0) + row_shift
    across = lax.broadcasted_iota(jnp.int32, (rows, columns), 1) + column_shift
    return jnp.where(down == across, 1.0, 0.0).astype(BF16)


def by_section(section, values):
    picked = values[0]
    for at in range(1, len(values)):
        if values[at] != values[at - 1]:
            picked = jnp.where(section >= at, values[at], picked)
    return picked


def kernel(
    sizes, tiles,
    slab_hbm, probe_hbm, amps_hbm, offsets_ref, counts_ref, tab_hbm,
    grad_ref, probe_out_ref,
    slab_ref, probe_ref, amps_ref, tab_ref,
    slab_parts, win, win_b, send_w, fields, cur, patch, send_g, recv_g, probe_acc, stage,
    send_f, recv_f, send_b, recv_b, pieces, sums, own_sum,
    sem_in, sem_sw, sem_rw, sem_sg, sem_rg, sem_sf, sem_rf, sem_sb, sem_rb, sem_ps, sem_pr, sem_zs, sem_zr, sem_go,
):
    n = probe_ref.shape[-1]
    side = slab_ref.shape[-1]
    slots = recv_g.shape[0]
    sections = sum(sizes)
    s = lax.axis_index("sec")
    t = lax.axis_index("tile")
    starts = [sum(sizes[:k]) for k in range(len(sizes))]
    group_of = [k for k, size in enumerate(sizes) for _ in range(size)]
    final = len(sizes) - 1
    size = by_section(s, [sizes[k] for k in group_of])
    start = by_section(s, [starts[k] for k in group_of])
    size_before = by_section(s, [sizes[max(k - 1, 0)] for k in group_of])
    start_before = by_section(s, [starts[max(k - 1, 0)] for k in group_of])
    size_after = by_section(s, [sizes[min(k + 1, final)] for k in group_of])
    start_after = by_section(s, [starts[min(k + 1, final)] for k in group_of])
    links_before = by_section(s, [max(1, sizes[max(k - 1, 0)] // sizes[k]) for k in group_of])
    links_after = by_section(s, [max(1, sizes[min(k + 1, final)] // sizes[k]) for k in group_of])
    rounds = by_section(s, [slots // sizes[k] for k in group_of])
    j = s - start
    first, last = s < starts[1], s >= starts[final]
    heads = sizes[0]

    inputs = [
        pltpu.make_async_copy(source, target, sem_in.at[at])
        for at, (source, target) in enumerate(
            ((slab_hbm, slab_ref), (tab_hbm, tab_ref), (probe_hbm, probe_ref), (amps_hbm, amps_ref)))
    ]
    for copy in inputs:
        copy.start()

    barrier = pltpu.get_barrier_semaphore()

    def greet(sec, tile):
        pl.semaphore_signal(barrier, inc=1, device_id=(sec, tile), device_id_type=MESH)

    for other in range(max(sizes)):
        @pl.when((other < size) & (other != j))
        def _():
            greet(start + other, t)

        @pl.when(jnp.logical_not(first) & (other < links_before))
        def _():
            greet(start_before + (j + size * other) % size_before, t)

        @pl.when(jnp.logical_not(last) & (other < links_after))
        def _():
            greet(start_after + (j + size * other) % size_after, t)

    per = sections // heads
    strangers = [
        int(k > 0 and not (k == 1 and (x - starts[1]) % heads == x // per)) for x, k in enumerate(group_of)]
    from_strangers = [sum(strangers[x * per:(x + 1) * per]) if x < heads else 0 for x in range(sections)]
    summer = s // per

    @pl.when(by_section(s, strangers) == 1)
    def _():
        greet(summer, t)

    @pl.when(first)
    def _():
        def greet_tile(step, carry):
            for member in range(heads):
                greet(member, (t + step) % tiles)
            return carry

        lax.fori_loop(1, tiles, greet_tile, 0)

    greetings = size - 1
    greetings += jnp.where(first, 0, links_before) + jnp.where(last, 0, links_after)
    greetings += jnp.where(first, (tiles - 1) * heads, 0) + by_section(s, from_strangers)

    grad_ref[...] = jnp.zeros_like(grad_ref)
    probe_acc[...] = jnp.zeros_like(probe_acc)

    planes = [(l, c) for l in range(2) for c in range(2)]
    inputs[0].wait()
    for at, (l, c) in enumerate(planes):
        high, low = split(slab_ref[l, c])
        slab_parts[:, at * side:(at + 1) * side] = high
        shift = (at + len(planes)) * side
        slab_parts[:, shift:shift + side] = low

    def cut(p, target, parts):
        rows = one_hot(n, side, offsets_ref[p, 0], 0)
        columns = one_hot(side, n, 0, offsets_ref[p, 1])
        for at, (l, c) in enumerate(planes):
            value = None
            for part in range(at, at + parts * len(planes), len(planes)):
                strip = dot(rows, slab_parts[:, part * side:(part + 1) * side]).astype(BF16)
                term = dot(strip, columns)
                value = term if value is None else value + term
            target[l, c] = value.astype(target.dtype)

    def place(p):
        rows = one_hot(side, n, 0, offsets_ref[p, 0])
        columns = one_hot(n, side, offsets_ref[p, 1], 0)
        for l, c in planes:
            strip = dot(recv_g[p, l, c], columns).astype(BF16)
            grad_ref[l, c] += dot(rows, strip)

    def copy_w(p):
        return pltpu.make_async_remote_copy(
            src_ref=send_w.at[p], dst_ref=win_b.at[(p // size) * size + j], send_sem=sem_sw.at[p],
            recv_sem=sem_rw.at[(p // size) * size + j], device_id=(start + p % size, t), device_id_type=MESH)

    def window_arrival(pair, owner):
        return pltpu.make_async_remote_copy(
            src_ref=send_w.at[0], dst_ref=win_b.at[pair], send_sem=sem_sw.at[0],
            recv_sem=sem_rw.at[pair], device_id=(start + owner, t), device_id_type=MESH)

    def copy_g(p, owner):
        pair = (p // size) * size + owner
        return pltpu.make_async_remote_copy(
            src_ref=send_g.at[pair], dst_ref=recv_g.at[p], send_sem=sem_sg.at[pair],
            recv_sem=sem_rg.at[p], device_id=(start + owner, t), device_id_type=MESH)

    def copy_f(p, m):
        return pltpu.make_async_remote_copy(
            src_ref=send_f.at[p, m], dst_ref=recv_f.at[p, m], send_sem=sem_sf.at[p, m], recv_sem=sem_rf.at[p, m],
            device_id=(start_after + p % size_after, t), device_id_type=MESH)

    def copy_b(p, m):
        return pltpu.make_async_remote_copy(
            src_ref=send_b.at[p, m], dst_ref=recv_b.at[p, m], send_sem=sem_sb.at[p, m], recv_sem=sem_rb.at[p, m],
            device_id=(start_before + p % size_before, t), device_id_type=MESH)

    def cut_round(i):
        def one(step, carry):
            member = (j + step) % size
            p = i * size + member

            @pl.when(step < size)
            def _():
                cut(p, send_w.at[p], 1)
                copy_w(p).start()

            @pl.when(step == size)
            def _():
                cut(p, win.at[i * size + j], 2)

            return carry

        lax.fori_loop(1, size + 1, one, 0)

    pl.semaphore_wait(barrier, greetings)
    cut_round(0)

    def cut_ahead(i, carry):
        cut_round(i)
        return carry

    lax.fori_loop(1, jnp.where(first, 1, rounds), cut_ahead, 0)

    for copy in inputs[1:]:
        copy.wait()

    def forward(i, modes):
        fresh = True if len(modes) == 2 else modes[0] == 0
        p = i * size + j
        base = i * size * 2

        @pl.when(first)
        def _():
            for m in modes:
                fields[base, m] = probe_ref[m]

        @pl.when(jnp.logical_not(first))
        def _():
            for m in modes:
                copy_f(p, m).wait_recv()
                fields[base, m] = recv_f[p, m].astype(F32)

        def slices(owner, carry):
            @pl.when((owner != j) & fresh)
            def _():
                pair = i * size + owner
                window_arrival(pair, owner).wait_recv()
                win[pair] = win_b[pair].astype(F32)

            for half in range(2):
                at = base + 2 * owner + half
                tr, ti = win[i * size + owner, half, 0], win[i * size + owner, half, 1]
                results = []
                for m in modes:
                    re, im = fields[at, m, 0], fields[at, m, 1]
                    results.append(two_sided(tab_ref, 0, 2, tr * re - ti * im, tr * im + ti * re))
                for m, result in zip(modes, results):
                    fields[at + 1, m, 0], fields[at + 1, m, 1] = result
            return carry

        lax.fori_loop(0, size, slices, 0)
        end = base + 2 * size

        @pl.when(jnp.logical_not(last))
        def _():
            for m in modes:
                send_f[p, m] = fields[end, m].astype(BF16)
                copy_f(p, m).start()

        if len(modes) == 2:
            @pl.when(last)
            def _():
                far(p, end)

    def far(p, end):
        spectrum = [two_sided(tab_ref, 4, 6, fields[end, m, 0], fields[end, m, 1]) for m in range(2)]
        intensity = sum(re * re + im * im for re, im in spectrum)
        modelled = jnp.sqrt(intensity + 0.25)
        live = jnp.where(p < counts_ref[0], 2.0, 0.0)
        factor = live * (1.0 - amps_ref[p].astype(F32) / modelled)
        for m, (re, im) in enumerate(spectrum):
            cur[m, 0], cur[m, 1] = two_sided(tab_ref, 6, 4, factor * re, factor * im)

    def backward(i, modes):
        whole = True if len(modes) == 2 else modes[0] == 1
        p = i * size + j
        base = i * size * 2

        @pl.when(jnp.logical_not(last))
        def _():
            for m in modes:
                copy_b(p, m).wait_recv()
                cur[m] = recv_b[p, m].astype(F32)

        def slices(step, carry):
            owner = size - 1 - step
            for half in (1, 0):
                at = base + 2 * owner + half
                tr, ti = win[i * size + owner, half, 0], win[i * size + owner, half, 1]
                middle = [two_sided(tab_ref, 2, 0, cur[m, 0], cur[m, 1]) for m in modes]
                piece_re = piece_im = 0.0
                for m, (re, im) in zip(modes, middle):
                    xr, xi = fields[at, m, 0], fields[at, m, 1]
                    piece_re += xr * re + xi * im
                    piece_im += xr * im - xi * re
                    cur[m, 0] = tr * re + ti * im
                    cur[m, 1] = tr * im - ti * re
                piece = (piece_re, piece_im)
                if len(modes) == 2:
                    patch[half, 0], patch[half, 1] = [part.astype(BF16) for part in piece]
                else:
                    @pl.when(modes[0] == 0)
                    def _():
                        for c in range(2):
                            fields[at, 0, c] = piece[c]

                    @pl.when(modes[0] == 1)
                    def _():
                        for c in range(2):
                            patch[half, c] = (fields[at, 0, c] + piece[c]).astype(BF16)

            @pl.when((owner == j) & whole)
            def _():
                recv_g[p] = patch[...]

            @pl.when((owner != j) & whole)
            def _():
                send_g[i * size + owner] = patch[...]

                @pl.when(first)
                def _():
                    copy_g(p, owner).start()

            return carry

        lax.fori_loop(0, size, slices, 0)

        @pl.when(jnp.logical_not(first))
        def _():
            for m in modes:
                send_b[p, m] = cur[m].astype(BF16)
                copy_b(p, m).start()

        @pl.when(first)
        def _():
            for m in modes:
                for c in range(2):
                    probe_acc[pl.ds(pl.multiple_of((2 * m + c) * n, n), n)] += cur[m, c]

    def send_patches():
        @pl.when(j == size - 1)
        def _():
            for m in range(2):
                copy_b((rounds - 1) * size + j, m).wait_send()

            def allow(step, carry):
                pl.semaphore_signal(
                    sem_go, inc=1, device_id=(start + (j + step) % size, t), device_id_type=MESH)
                return carry

            lax.fori_loop(1, size, allow, 0)

        @pl.when(j < size - 1)
        def _():
            pl.semaphore_wait(sem_go, 1)

        def of_round(i, carry):
            def one(step, inner):
                copy_g(i * size + j, (j + step) % size).start()
                return inner

            return lax.fori_loop(1, size, one, carry)

        lax.fori_loop(0, rounds, of_round, 0)

    def place_round(i):
        def one(step, carry):
            member = (j + step) % size
            p = i * size + member

            @pl.when(step > 0)
            def _():
                pltpu.make_async_remote_copy(
                    src_ref=send_g.at[0], dst_ref=recv_g.at[p], send_sem=sem_sg.at[0],
                    recv_sem=sem_rg.at[p], device_id=(start + member, t), device_id_type=MESH).wait_recv()

            place(p)
            return carry

        lax.fori_loop(0, size, one, 0)

    alone = (size <= ALONE) & jnp.logical_not(last)

    def by_modes(work, i):
        @pl.when(alone)
        def _():
            def one(m, carry):
                work(i, (m,))
                return carry

            lax.fori_loop(0, 2, one, 0)

        @pl.when(jnp.logical_not(alone))
        def _():
            work(i, (0, 1))

    def turn(u, carry):
        onward = jnp.where(last, u % 2 == 0, u < rounds)

        @pl.when(onward)
        def _():
            i = jnp.where(last, u // 2, u)
            by_modes(forward, i)

            @pl.when(first & (i + 1 < rounds))
            def _():
                cut_round(i + 1)

        @pl.when(jnp.logical_not(onward))
        def _():
            i = jnp.where(last, u // 2, u - rounds)
            by_modes(backward, i)

        return carry

    lax.fori_loop(0, 2 * rounds, turn, 0)

    lines = 4 * n // sections
    share = lines // tiles

    def copy_p(member, other):
        return pltpu.make_async_remote_copy(
            src_ref=stage.at[other, :, pl.ds(member * per, per)], dst_ref=pieces.at[j * tiles + t],
            send_sem=sem_ps.at[member * tiles + other], recv_sem=sem_pr.at[j * tiles + t],
            device_id=(member, other), device_id_type=MESH)

    def arrival_p(slot):
        return pltpu.make_async_remote_copy(
            src_ref=stage.at[0, :, pl.ds(0, per)], dst_ref=pieces.at[slot], send_sem=sem_ps.at[0],
            recv_sem=sem_pr.at[slot], device_id=(s, t), device_id_type=MESH)

    def copy_z(at):
        return pltpu.make_async_remote_copy(
            src_ref=sums.at[at], dst_ref=own_sum, send_sem=sem_zs.at[at], recv_sem=sem_zr,
            device_id=(j * per + at, t), device_id_type=MESH)

    def each_piece(act):
        def one(step, carry):
            other = (t + step) % tiles
            for member in range(heads):
                @pl.when((step > 0) | (member != j))
                def _():
                    act(copy_p(member, other))

            return carry

        lax.fori_loop(0, tiles, one, 0)

    @pl.when(first)
    def _():
        for other in range(tiles):
            for k in range(share):
                stage[other, k] = probe_acc[pl.ds(other * share + k, sections, stride=lines), :]
        each_piece(lambda copy: copy.start())
        pieces[j * tiles + t] = stage[t, :, pl.ds(j * per, per)]

    @pl.when(jnp.logical_not(first))
    def _():
        send_patches()

    def placing(i, carry):
        place_round(i)
        return carry

    lax.fori_loop(0, rounds, placing, 0)

    @pl.when(first)
    def _():
        def arrive(slot, carry):
            @pl.when(slot != j * tiles + t)
            def _():
                arrival_p(slot).wait_recv()

            return carry

        lax.fori_loop(0, heads * tiles, arrive, 0)
        total = pieces[0]
        for slot in range(1, heads * tiles):
            total = total + pieces[slot]
        for at in range(per):
            sums[at] = jnp.broadcast_to(total[:, at], sums.shape[1:])
        for at in range(per):
            @pl.when(j * per + at != s)
            def _():
                copy_z(at).start()

            @pl.when(j * per + at == s)
            def _():
                own_sum[...] = sums[at]

    @pl.when(summer != s)
    def _():
        pltpu.make_async_remote_copy(
            src_ref=sums.at[0], dst_ref=own_sum, send_sem=sem_zs.at[0], recv_sem=sem_zr,
            device_id=(summer, t), device_id_type=MESH).wait_recv()

    probe_out_ref[...] = own_sum[0:share]

    @pl.when(first)
    def _():
        each_piece(lambda copy: copy.wait_send())
        for at in range(per):
            @pl.when(j * per + at != s)
            def _():
                copy_z(at).wait_send()

    def sent(p, carry):
        @pl.when(p % size != j)
        def _():
            copy_w(p).wait_send()

        @pl.when(p % size == j)
        def _():
            for m in range(2):
                @pl.when(jnp.logical_not(last))
                def _():
                    copy_f(p, m).wait_send()

                @pl.when(jnp.logical_not(first) & ((j < size - 1) | (p < slots - 1)))
                def _():
                    copy_b(p, m).wait_send()

            def sent_piece(owner, inner):
                @pl.when(owner != j)
                def _():
                    copy_g(p, owner).wait_send()

                return inner

            lax.fori_loop(0, size, sent_piece, 0)

        return carry

    lax.fori_loop(0, slots, sent, 0)


ALONE = 2
GROUPS = {16: (2, 2, 4, 8), 8: (2, 2, 4), 4: (2, 2)}


def shards(sections, tiles, slab, probe, amplitudes, offsets, counts):
    layers, _, side, _ = slab.shape
    n = probe.shape[-1]
    slots = offsets.shape[0]
    sizes = GROUPS[sections]
    lines = 4 * n // sections
    share = lines // tiles
    per = sections // sizes[0]
    sum_rows = max(8, share)
    hbm = pl.BlockSpec(memory_space=pltpu.HBM)
    vmem = pl.BlockSpec(memory_space=pltpu.VMEM)
    smem = pl.BlockSpec(memory_space=pltpu.SMEM)
    tab = jnp.asarray(tables(n))
    window = (layers, 2, n, n)
    wave = (slots, 2, 2, n, n)
    dma = pltpu.SemaphoreType.DMA
    grad, probe_grad = pl.pallas_call(
        functools.partial(kernel, sizes, tiles),
        out_shape=(
            jax.ShapeDtypeStruct(slab.shape, F32),
            jax.ShapeDtypeStruct((share, n), F32),
        ),
        in_specs=[hbm, hbm, hbm, smem, smem, hbm],
        out_specs=(vmem, vmem),
        scratch_shapes=[
            pltpu.VMEM(slab.shape, F32),
            pltpu.VMEM(probe.shape, F32),
            pltpu.VMEM(amplitudes.shape, BF16),
            pltpu.VMEM(tab.shape, BF16),
            pltpu.VMEM((side, side * layers * 4), BF16),
            pltpu.VMEM((slots,) + window, F32),
            pltpu.VMEM((slots,) + window, BF16),
            pltpu.VMEM((slots,) + window, BF16),
            pltpu.VMEM((slots * layers + 1, 2, 2, n, n), F32),
            pltpu.VMEM((2, 2, n, n), F32),
            pltpu.VMEM(window, BF16),
            pltpu.VMEM((slots,) + window, BF16),
            pltpu.VMEM((slots,) + window, BF16),
            pltpu.VMEM((4 * n, n), F32),
            pltpu.VMEM((tiles, share, sections, n), F32),
            pltpu.VMEM(wave, BF16),
            pltpu.VMEM(wave, BF16),
            pltpu.VMEM(wave, BF16),
            pltpu.VMEM(wave, BF16),
            pltpu.VMEM((sizes[0] * tiles, share, per, n), F32),
            pltpu.VMEM((per, sum_rows, n), F32),
            pltpu.VMEM((sum_rows, n), F32),
            dma((4,)),
            dma((slots,)), dma((slots,)),
            dma((slots,)), dma((slots,)),
            dma((slots, 2)), dma((slots, 2)),
            dma((slots, 2)), dma((slots, 2)),
            dma((sizes[0] * tiles,)), dma((sizes[0] * tiles,)),
            dma((per,)), dma,
            pltpu.SemaphoreType.REGULAR,
        ],
        compiler_params=pltpu.CompilerParams(
            collective_id=0, has_side_effects=True, vmem_limit_bytes=56 * 1024 * 1024),
    )(slab, probe, amplitudes, offsets, counts, tab)
    return grad, probe_grad.reshape(-1)


def solution(mesh):
    body = functools.partial(shards, mesh.shape["sec"], mesh.shape["tile"])
    in_specs = (
        P("sec", None, "tile", None),
        P(),
        P("tile", None, None),
        P("tile", None),
        P("tile"),
    )
    out_specs = (P("sec", None, "tile", None), P(("sec", "tile")))
    return jax.shard_map(body, mesh=mesh, in_specs=in_specs, out_specs=out_specs, check_vma=False)
```

```python
import functools

import jax
import jax.numpy as jnp
import ml_dtypes
import numpy as np
from jax import lax
from jax.experimental import pallas as pl
from jax.experimental.pallas import tpu as pltpu
from jax.sharding import PartitionSpec as P

PHASE_SCALE = 20.0
F32 = jnp.float32
BF16 = jnp.bfloat16
MESH = pl.DeviceIdType.MESH


def real_forms(matrix):
    re, im = matrix.real, matrix.imag
    left = np.block([[re, -im], [im, re]])
    right = np.block([[re, im], [-im, re]])
    pieces = []
    for table in (right, left):
        table = table.astype(np.float32)
        high = table.astype(ml_dtypes.bfloat16)
        low = (table - high.astype(np.float32)).astype(ml_dtypes.bfloat16)
        pieces += [high, low]
    return pieces


def tables(length):
    index = np.arange(length)
    dft = np.exp(-2j * np.pi * (np.outer(index, index) % length) / length)
    frequency = np.where(index < (length + 1) // 2, index, index - length) / length
    phases = np.exp(-1j * PHASE_SCALE * frequency * frequency)
    propagator = (dft.conj() @ (phases[:, None] * dft)) / length
    return np.stack(real_forms(propagator) + real_forms(dft / np.sqrt(length)))


def split(value):
    high = value.astype(BF16)
    return high, (value - high.astype(F32)).astype(BF16)


def dot(a, b):
    return jnp.dot(a, b, preferred_element_type=F32)


def two_sided(tab_ref, right, left, re, im):
    n = re.shape[0]
    high, low = split(jnp.concatenate([re, im], axis=1))
    right_high = tab_ref[right]
    half = dot(high, right_high) + dot(low, right_high) + dot(high, tab_ref[right + 1])
    high, low = split(jnp.concatenate([half[:, :n], half[:, n:]], axis=0))
    both = dot(tab_ref[left], jnp.concatenate([high, low], axis=1))
    out = both[:, :n] + both[:, n:] + dot(tab_ref[left + 1], high)
    return out[:n], out[n:]


def one_hot(rows, columns, row_shift, column_shift):
    down = lax.broadcasted_iota(jnp.int32, (rows, columns), 0) + row_shift
    across = lax.broadcasted_iota(jnp.int32, (rows, columns), 1) + column_shift
    return jnp.where(down == across, 1.0, 0.0).astype(BF16)


def by_section(section, values):
    picked = values[0]
    for at in range(1, len(values)):
        if values[at] != values[at - 1]:
            picked = jnp.where(section >= at, values[at], picked)
    return picked


def kernel(
    sizes, tiles,
    slab_hbm, probe_hbm, amps_hbm, offsets_ref, counts_ref, tab_hbm,
    grad_ref, probe_out_ref,
    slab_ref, probe_ref, amps_ref, tab_ref,
    slab_parts, win, win_b, send_w, fields, cur, patch, send_g, recv_g, probe_acc, stage,
    send_f, recv_f, send_b, recv_b, pieces, sums, own_sum,
    sem_in, sem_sw, sem_rw, sem_sg, sem_rg, sem_sf, sem_rf, sem_sb, sem_rb, sem_ps, sem_pr, sem_zs, sem_zr, sem_go,
):
    n = probe_ref.shape[-1]
    side = slab_ref.shape[-1]
    slots = recv_g.shape[0]
    sections = sum(sizes)
    s = lax.axis_index("sec")
    t = lax.axis_index("tile")
    starts = [sum(sizes[:k]) for k in range(len(sizes))]
    group_of = [k for k, size in enumerate(sizes) for _ in range(size)]
    final = len(sizes) - 1
    size = by_section(s, [sizes[k] for k in group_of])
    start = by_section(s, [starts[k] for k in group_of])
    size_before = by_section(s, [sizes[max(k - 1, 0)] for k in group_of])
    start_before = by_section(s, [starts[max(k - 1, 0)] for k in group_of])
    size_after = by_section(s, [sizes[min(k + 1, final)] for k in group_of])
    start_after = by_section(s, [starts[min(k + 1, final)] for k in group_of])
    links_before = by_section(s, [max(1, sizes[max(k - 1, 0)] // sizes[k]) for k in group_of])
    links_after = by_section(s, [max(1, sizes[min(k + 1, final)] // sizes[k]) for k in group_of])
    rounds = by_section(s, [slots // sizes[k] for k in group_of])
    j = s - start
    first, last = s < starts[1], s >= starts[final]
    heads = sizes[0]

    inputs = [
        pltpu.make_async_copy(source, target, sem_in.at[at])
        for at, (source, target) in enumerate(
            ((slab_hbm, slab_ref), (tab_hbm, tab_ref), (probe_hbm, probe_ref), (amps_hbm, amps_ref)))
    ]
    for copy in inputs:
        copy.start()

    barrier = pltpu.get_barrier_semaphore()

    def greet(sec, tile):
        pl.semaphore_signal(barrier, inc=1, device_id=(sec, tile), device_id_type=MESH)

    for other in range(max(sizes)):
        @pl.when((other < size) & (other != j))
        def _():
            greet(start + other, t)

        @pl.when(jnp.logical_not(first) & (other < links_before))
        def _():
            greet(start_before + (j + size * other) % size_before, t)

        @pl.when(jnp.logical_not(last) & (other < links_after))
        def _():
            greet(start_after + (j + size * other) % size_after, t)

    per = sections // heads
    strangers = [
        int(k > 0 and not (k == 1 and (x - starts[1]) % heads == x // per)) for x, k in enumerate(group_of)]
    from_strangers = [sum(strangers[x * per:(x + 1) * per]) if x < heads else 0 for x in range(sections)]
    summer = s // per

    @pl.when(by_section(s, strangers) == 1)
    def _():
        greet(summer, t)

    @pl.when(first)
    def _():
        def greet_tile(step, carry):
            for member in range(heads):
                greet(member, (t + step) % tiles)
            return carry

        lax.fori_loop(1, tiles, greet_tile, 0)

    greetings = size - 1
    greetings += jnp.where(first, 0, links_before) + jnp.where(last, 0, links_after)
    greetings += jnp.where(first, (tiles - 1) * heads, 0) + by_section(s, from_strangers)

    grad_ref[...] = jnp.zeros_like(grad_ref)
    probe_acc[...] = jnp.zeros_like(probe_acc)

    planes = [(l, c) for l in range(2) for c in range(2)]
    inputs[0].wait()
    for at, (l, c) in enumerate(planes):
        high, low = split(slab_ref[l, c])
        slab_parts[:, at * side:(at + 1) * side] = high
        shift = (at + len(planes)) * side
        slab_parts[:, shift:shift + side] = low

    def cut(p, target, parts):
        rows = one_hot(n, side, offsets_ref[p, 0], 0)
        columns = one_hot(side, n, 0, offsets_ref[p, 1])
        for at, (l, c) in enumerate(planes):
            value = None
            for part in range(at, at + parts * len(planes), len(planes)):
                strip = dot(rows, slab_parts[:, part * side:(part + 1) * side]).astype(BF16)
                term = dot(strip, columns)
                value = term if value is None else value + term
            target[l, c] = value.astype(target.dtype)

    def place(p):
        rows = one_hot(side, n, 0, offsets_ref[p, 0])
        columns = one_hot(n, side, offsets_ref[p, 1], 0)
        for l, c in planes:
            strip = dot(recv_g[p, l, c], columns).astype(BF16)
            grad_ref[l, c] += dot(rows, strip)

    def copy_w(p):
        return pltpu.make_async_remote_copy(
            src_ref=send_w.at[p], dst_ref=win_b.at[(p // size) * size + j], send_sem=sem_sw.at[p],
            recv_sem=sem_rw.at[(p // size) * size + j], device_id=(start + p % size, t), device_id_type=MESH)

    def window_arrival(pair, owner):
        return pltpu.make_async_remote_copy(
            src_ref=send_w.at[0], dst_ref=win_b.at[pair], send_sem=sem_sw.at[0],
            recv_sem=sem_rw.at[pair], device_id=(start + owner, t), device_id_type=MESH)

    def copy_g(p, owner):
        pair = (p // size) * size + owner
        return pltpu.make_async_remote_copy(
            src_ref=send_g.at[pair], dst_ref=recv_g.at[p], send_sem=sem_sg.at[pair],
            recv_sem=sem_rg.at[p], device_id=(start + owner, t), device_id_type=MESH)

    def copy_f(p, m):
        return pltpu.make_async_remote_copy(
            src_ref=send_f.at[p, m], dst_ref=recv_f.at[p, m], send_sem=sem_sf.at[p, m], recv_sem=sem_rf.at[p, m],
            device_id=(start_after + p % size_after, t), device_id_type=MESH)

    def copy_b(p, m):
        return pltpu.make_async_remote_copy(
            src_ref=send_b.at[p, m], dst_ref=recv_b.at[p, m], send_sem=sem_sb.at[p, m], recv_sem=sem_rb.at[p, m],
            device_id=(start_before + p % size_before, t), device_id_type=MESH)

    def cut_round(i):
        def one(step, carry):
            member = (j + step) % size
            p = i * size + member

            @pl.when(step < size)
            def _():
                cut(p, send_w.at[p], 1)
                copy_w(p).start()

            @pl.when(step == size)
            def _():
                cut(p, win.at[i * size + j], 2)

            return carry

        lax.fori_loop(1, size + 1, one, 0)

    pl.semaphore_wait(barrier, greetings)
    cut_round(0)

    def cut_ahead(i, carry):
        cut_round(i)
        return carry

    lax.fori_loop(1, jnp.where(first, 1, rounds), cut_ahead, 0)

    for copy in inputs[1:]:
        copy.wait()

    def forward(i, modes):
        fresh = True if len(modes) == 2 else modes[0] == 0
        p = i * size + j
        base = i * size * 2

        @pl.when(first)
        def _():
            for m in modes:
                fields[base, m] = probe_ref[m]

        @pl.when(jnp.logical_not(first))
        def _():
            for m in modes:
                copy_f(p, m).wait_recv()
                fields[base, m] = recv_f[p, m].astype(F32)

        def slices(owner, carry):
            @pl.when((owner != j) & fresh)
            def _():
                pair = i * size + owner
                window_arrival(pair, owner).wait_recv()
                win[pair] = win_b[pair].astype(F32)

            for half in range(2):
                at = base + 2 * owner + half
                tr, ti = win[i * size + owner, half, 0], win[i * size + owner, half, 1]
                results = []
                for m in modes:
                    re, im = fields[at, m, 0], fields[at, m, 1]
                    results.append(two_sided(tab_ref, 0, 2, tr * re - ti * im, tr * im + ti * re))
                for m, result in zip(modes, results):
                    fields[at + 1, m, 0], fields[at + 1, m, 1] = result
            return carry

        lax.fori_loop(0, size, slices, 0)
        end = base + 2 * size

        @pl.when(jnp.logical_not(last))
        def _():
            for m in modes:
                send_f[p, m] = fields[end, m].astype(BF16)
                copy_f(p, m).start()

        if len(modes) == 2:
            @pl.when(last)
            def _():
                far(p, end)

    def far(p, end):
        spectrum = [two_sided(tab_ref, 4, 6, fields[end, m, 0], fields[end, m, 1]) for m in range(2)]
        intensity = sum(re * re + im * im for re, im in spectrum)
        modelled = jnp.sqrt(intensity + 0.25)
        live = jnp.where(p < counts_ref[0], 2.0, 0.0)
        factor = live * (1.0 - amps_ref[p].astype(F32) / modelled)
        for m, (re, im) in enumerate(spectrum):
            cur[m, 0], cur[m, 1] = two_sided(tab_ref, 6, 4, factor * re, factor * im)

    def backward(i, modes):
        whole = True if len(modes) == 2 else modes[0] == 1
        p = i * size + j
        base = i * size * 2

        @pl.when(jnp.logical_not(last))
        def _():
            for m in modes:
                copy_b(p, m).wait_recv()
                cur[m] = recv_b[p, m].astype(F32)

        def slices(step, carry):
            owner = size - 1 - step
            for half in (1, 0):
                at = base + 2 * owner + half
                tr, ti = win[i * size + owner, half, 0], win[i * size + owner, half, 1]
                middle = [two_sided(tab_ref, 2, 0, cur[m, 0], cur[m, 1]) for m in modes]
                piece_re = piece_im = 0.0
                for m, (re, im) in zip(modes, middle):
                    xr, xi = fields[at, m, 0], fields[at, m, 1]
                    piece_re += xr * re + xi * im
                    piece_im += xr * im - xi * re
                    cur[m, 0] = tr * re + ti * im
                    cur[m, 1] = tr * im - ti * re
                piece = (piece_re, piece_im)
                if len(modes) == 2:
                    patch[half, 0], patch[half, 1] = [part.astype(BF16) for part in piece]
                else:
                    @pl.when(modes[0] == 0)
                    def _():
                        for c in range(2):
                            fields[at, 0, c] = piece[c]

                    @pl.when(modes[0] == 1)
                    def _():
                        for c in range(2):
                            patch[half, c] = (fields[at, 0, c] + piece[c]).astype(BF16)

            @pl.when((owner == j) & whole)
            def _():
                recv_g[p] = patch[...]

            @pl.when((owner != j) & whole)
            def _():
                send_g[i * size + owner] = patch[...]

                @pl.when(first)
                def _():
                    copy_g(p, owner).start()

            return carry

        lax.fori_loop(0, size, slices, 0)

        @pl.when(jnp.logical_not(first))
        def _():
            for m in modes:
                send_b[p, m] = cur[m].astype(BF16)
                copy_b(p, m).start()

        @pl.when(first)
        def _():
            for m in modes:
                for c in range(2):
                    probe_acc[pl.ds(pl.multiple_of((2 * m + c) * n, n), n)] += cur[m, c]

    def send_patches():
        @pl.when(j == size - 1)
        def _():
            for m in range(2):
                copy_b((rounds - 1) * size + j, m).wait_send()

            def allow(step, carry):
                pl.semaphore_signal(
                    sem_go, inc=1, device_id=(start + (j + step) % size, t), device_id_type=MESH)
                return carry

            lax.fori_loop(1, size, allow, 0)

        @pl.when(j < size - 1)
        def _():
            pl.semaphore_wait(sem_go, 1)

        def of_round(i, carry):
            def one(step, inner):
                copy_g(i * size + j, (j + step) % size).start()
                return inner

            return lax.fori_loop(1, size, one, carry)

        lax.fori_loop(0, rounds, of_round, 0)

    def place_round(i):
        def one(step, carry):
            member = (j + step) % size
            p = i * size + member

            @pl.when(step > 0)
            def _():
                pltpu.make_async_remote_copy(
                    src_ref=send_g.at[0], dst_ref=recv_g.at[p], send_sem=sem_sg.at[0],
                    recv_sem=sem_rg.at[p], device_id=(start + member, t), device_id_type=MESH).wait_recv()

            place(p)
            return carry

        lax.fori_loop(0, size, one, 0)

    alone = (size <= ALONE) & jnp.logical_not(last)

    def by_modes(work, i):
        @pl.when(alone)
        def _():
            def one(m, carry):
                work(i, (m,))
                return carry

            lax.fori_loop(0, 2, one, 0)

        @pl.when(jnp.logical_not(alone))
        def _():
            work(i, (0, 1))

    def turn(u, carry):
        onward = jnp.where(last, u % 2 == 0, u < rounds)

        @pl.when(onward)
        def _():
            i = jnp.where(last, u // 2, u)
            by_modes(forward, i)

            @pl.when(first & (i + 1 < rounds))
            def _():
                cut_round(i + 1)

        @pl.when(jnp.logical_not(onward))
        def _():
            i = jnp.where(last, u // 2, u - rounds)
            by_modes(backward, i)

        return carry

    lax.fori_loop(0, 2 * rounds, turn, 0)

    lines = 4 * n // sections
    share = lines // tiles

    def copy_p(member, other):
        return pltpu.make_async_remote_copy(
            src_ref=stage.at[other, :, pl.ds(member * per, per)], dst_ref=pieces.at[j * tiles + t],
            send_sem=sem_ps.at[member * tiles + other], recv_sem=sem_pr.at[j * tiles + t],
            device_id=(member, other), device_id_type=MESH)

    def arrival_p(slot):
        return pltpu.make_async_remote_copy(
            src_ref=stage.at[0, :, pl.ds(0, per)], dst_ref=pieces.at[slot], send_sem=sem_ps.at[0],
            recv_sem=sem_pr.at[slot], device_id=(s, t), device_id_type=MESH)

    def copy_z(at):
        return pltpu.make_async_remote_copy(
            src_ref=sums.at[at], dst_ref=own_sum, send_sem=sem_zs.at[at], recv_sem=sem_zr,
            device_id=(j * per + at, t), device_id_type=MESH)

    def each_piece(act):
        def one(step, carry):
            other = (t + step) % tiles
            for member in range(heads):
                @pl.when((step > 0) | (member != j))
                def _():
                    act(copy_p(member, other))

            return carry

        lax.fori_loop(0, tiles, one, 0)

    @pl.when(first)
    def _():
        for other in range(tiles):
            for k in range(share):
                stage[other, k] = probe_acc[pl.ds(other * share + k, sections, stride=lines), :]
        each_piece(lambda copy: copy.start())
        pieces[j * tiles + t] = stage[t, :, pl.ds(j * per, per)]

    @pl.when(jnp.logical_not(first))
    def _():
        send_patches()

    def placing(i, carry):
        place_round(i)
        return carry

    lax.fori_loop(0, rounds, placing, 0)

    @pl.when(first)
    def _():
        def arrive(slot, carry):
            @pl.when(slot != j * tiles + t)
            def _():
                arrival_p(slot).wait_recv()

            return carry

        lax.fori_loop(0, heads * tiles, arrive, 0)
        total = pieces[0]
        for slot in range(1, heads * tiles):
            total = total + pieces[slot]
        for at in range(per):
            sums[at] = jnp.broadcast_to(total[:, at], sums.shape[1:])
        for at in range(per):
            @pl.when(j * per + at != s)
            def _():
                copy_z(at).start()

            @pl.when(j * per + at == s)
            def _():
                own_sum[...] = sums[at]

    @pl.when(summer != s)
    def _():
        pltpu.make_async_remote_copy(
            src_ref=sums.at[0], dst_ref=own_sum, send_sem=sem_zs.at[0], recv_sem=sem_zr,
            device_id=(summer, t), device_id_type=MESH).wait_recv()

    probe_out_ref[...] = own_sum[0:share]

    @pl.when(first)
    def _():
        each_piece(lambda copy: copy.wait_send())
        for at in range(per):
            @pl.when(j * per + at != s)
            def _():
                copy_z(at).wait_send()

    def sent(p, carry):
        @pl.when(p % size != j)
        def _():
            copy_w(p).wait_send()

        @pl.when(p % size == j)
        def _():
            for m in range(2):
                @pl.when(jnp.logical_not(last))
                def _():
                    copy_f(p, m).wait_send()

                @pl.when(jnp.logical_not(first) & ((j < size - 1) | (p < slots - 1)))
                def _():
                    copy_b(p, m).wait_send()

            def sent_piece(owner, inner):
                @pl.when(owner != j)
                def _():
                    copy_g(p, owner).wait_send()

                return inner

            lax.fori_loop(0, size, sent_piece, 0)

        return carry

    lax.fori_loop(0, slots, sent, 0)


ALONE = 2
GROUPS = {16: (1, 1, 2, 4, 8), 8: (2, 2, 4), 4: (2, 2)}


def shards(sections, tiles, slab, probe, amplitudes, offsets, counts):
    layers, _, side, _ = slab.shape
    n = probe.shape[-1]
    slots = offsets.shape[0]
    sizes = GROUPS[sections]
    lines = 4 * n // sections
    share = lines // tiles
    per = sections // sizes[0]
    sum_rows = max(8, share)
    hbm = pl.BlockSpec(memory_space=pltpu.HBM)
    vmem = pl.BlockSpec(memory_space=pltpu.VMEM)
    smem = pl.BlockSpec(memory_space=pltpu.SMEM)
    tab = jnp.asarray(tables(n))
    window = (layers, 2, n, n)
    wave = (slots, 2, 2, n, n)
    dma = pltpu.SemaphoreType.DMA
    grad, probe_grad = pl.pallas_call(
        functools.partial(kernel, sizes, tiles),
        out_shape=(
            jax.ShapeDtypeStruct(slab.shape, F32),
            jax.ShapeDtypeStruct((share, n), F32),
        ),
        in_specs=[hbm, hbm, hbm, smem, smem, hbm],
        out_specs=(vmem, vmem),
        scratch_shapes=[
            pltpu.VMEM(slab.shape, F32),
            pltpu.VMEM(probe.shape, F32),
            pltpu.VMEM(amplitudes.shape, BF16),
            pltpu.VMEM(tab.shape, BF16),
            pltpu.VMEM((side, side * layers * 4), BF16),
            pltpu.VMEM((slots,) + window, F32),
            pltpu.VMEM((slots,) + window, BF16),
            pltpu.VMEM((slots,) + window, BF16),
            pltpu.VMEM((slots * layers + 1, 2, 2, n, n), F32),
            pltpu.VMEM((2, 2, n, n), F32),
            pltpu.VMEM(window, BF16),
            pltpu.VMEM((slots,) + window, BF16),
            pltpu.VMEM((slots,) + window, BF16),
            pltpu.VMEM((4 * n, n), F32),
            pltpu.VMEM((tiles, share, sections, n), F32),
            pltpu.VMEM(wave, BF16),
            pltpu.VMEM(wave, BF16),
            pltpu.VMEM(wave, BF16),
            pltpu.VMEM(wave, BF16),
            pltpu.VMEM((sizes[0] * tiles, share, per, n), F32),
            pltpu.VMEM((per, sum_rows, n), F32),
            pltpu.VMEM((sum_rows, n), F32),
            dma((4,)),
            dma((slots,)), dma((slots,)),
            dma((slots,)), dma((slots,)),
            dma((slots, 2)), dma((slots, 2)),
            dma((slots, 2)), dma((slots, 2)),
            dma((sizes[0] * tiles,)), dma((sizes[0] * tiles,)),
            dma((per,)), dma,
            pltpu.SemaphoreType.REGULAR,
        ],
        compiler_params=pltpu.CompilerParams(
            collective_id=0, has_side_effects=True, vmem_limit_bytes=56 * 1024 * 1024),
    )(slab, probe, amplitudes, offsets, counts, tab)
    return grad, probe_grad.reshape(-1)


def solution(mesh):
    body = functools.partial(shards, mesh.shape["sec"], mesh.shape["tile"])
    in_specs = (
        P("sec", None, "tile", None),
        P(),
        P("tile", None, None),
        P("tile", None),
        P("tile"),
    )
    out_specs = (P("sec", None, "tile", None), P(("sec", "tile")))
    return jax.shard_map(body, mesh=mesh, in_specs=in_specs, out_specs=out_specs, check_vma=False)
```
